512 devices in a mesh: dp: 64 (over z, y), tensor: 8 (over x, core).
Axes of the slice: x: 4, y: 4, z: 16, core: 2. Of those that a mesh axis runs over, the one named last changes fastest.
Arguments:
- patches: bfloat16 [16384, 1280], P('dp', 'tensor'), may hold values from -46 to 46
- send_counts: int32 [64, 64], replicated, may hold values from 0 to 4, as said below
- window_ids: int32 [128, 64], P('dp'), may hold values from 0 to 2, never falling along the last dimension, each value on 1 to 40 neighbouring positions
- token_shard: int32 [2048, 1], replicated, may hold values from 0 to 63; in each aligned block of 32 rows (0 to 31, 32 to 63, ...) at most 2 rows name the same one
- first_gain: float32 [1280], replicated, may hold values from 0.25 to 1.75
- qkv_weight: bfloat16 [1280, 3840], P(None, 'tensor'), may hold values from -1 to 1
- out_weight: bfloat16 [1280, 1280], P(None, 'tensor'), may hold values from -0.15625 to 0.15625
- merge_gain: float32 [1280], P('tensor'), may hold values from 0.25 to 1.75
- cotangent: bfloat16 [8192, 4, 1280], P('dp', None, 'tensor'), may hold values from -0.29882812 to 0.29882812
Outputs:
- merged_tokens: bfloat16 [8192, 4, 1280], P('dp', None, 'tensor')
- qkv_grad: bfloat16 [1280, 3840], P(None, 'tensor')
- out_grad: bfloat16 [1280, 1280], P(None, 'tensor')
- gain_grad: float32 [1280], P('tensor')
The draws below stay inside these ranges and needn't reach their ends.
Inputs may be any that keep to these rules, and one draw needn't show every extreme that they name: `send_counts`: entry [i, j] is the number of live rows that source i sends to owner j; every column sums to exactly 128 and holds one entry equal to 4. `window_ids`: ids never fall along a row; each row is one tile of 64 rows of the owner layout. `token_shard`: among the 32 tokens of one owner (aligned blocks of 32 rows) no shard is named more than 2 times.
All inputs are finite; a program needn't handle non-finite values.
Results may differ from the reference program's by a relative error of at most 0.023.
Values may be sent and summed in bfloat16 or wider, within the bound.
A program may use at most 64 MiB of HBM per device.

```python
import math
import jax
import jax.numpy as jnp
import numpy as np
from jax import lax

D = 1280
HEADS = 16
HD = 80
WIN = 64
ROWS_OWN = 128
ROWS_SRC = 256
ROWS = 8192
SLOT_CAP = 4
TOK = 32
TOKEN_CAP = 2
LM_DEV = 128
GROUP_FEAT = 160
N_DP = 64
N_TENSOR = 8


def draw_patches(key, part):
    key = jax.random.fold_in(key, 11)
    row_key, col_key, main_key = jax.random.split(key, 3)
    total_rows = N_DP * ROWS_SRC
    row_scale = jnp.exp(jax.random.uniform(row_key, (total_rows, 1), jnp.float32, -1.2, 1.1))
    ramp_pos = (jnp.arange(D, dtype=jnp.float32) + jax.random.uniform(col_key, (D,), jnp.float32)) / D
    col_scale = jnp.exp(-1.2 + 2.3 * ramp_pos)[None, :]
    sample = jax.random.normal(main_key, (total_rows, D), jnp.float32)
    sample = jnp.clip(sample, -5.0, 5.0)
    return (sample * row_scale * col_scale).astype(jnp.bfloat16)


def draw_send_counts(key, part):
    key = jax.random.fold_in(key, 23)
    perm_key, bin_key = jax.random.split(key)
    slot_total = N_DP * SLOT_CAP
    owner_keys = jax.random.split(perm_key, N_DP)
    shuffled = jax.vmap(lambda owner_key: jax.random.permutation(owner_key, slot_total))(owner_keys).astype(jnp.int32)
    full_bin = jax.random.randint(bin_key, (N_DP, 1), 0, N_DP).astype(jnp.int32)
    bin_of = (jnp.arange(slot_total, dtype=jnp.int32) // SLOT_CAP)[None, :]
    scored = shuffled + slot_total * (bin_of == full_bin).astype(jnp.int32)
    cutoff = lax.top_k(scored, ROWS_OWN)[0][:, ROWS_OWN - 1:ROWS_OWN]
    chosen = (scored >= cutoff).astype(jnp.int32)
    counts = jnp.sum(chosen.reshape(N_DP, N_DP, SLOT_CAP), axis=2).astype(jnp.int32)
    return counts.T


def draw_qkv_weight(key, part):
    key = jax.random.fold_in(key, 37)
    base_key = jax.random.fold_in(key, 0)
    matrix = jax.random.normal(base_key, (D, HEADS, 3, HD), jnp.float32) * D ** (-0.5)
    matrix = jnp.clip(matrix, -1.0, 1.0)
    return matrix.reshape(D, 3 * D).astype(jnp.bfloat16)


def steps_of(own_key, shape, cuts, least, high):
    loudness = 1.0
    for dim, parts in cuts:
        steps = jax.random.uniform(jax.random.fold_in(jax.random.fold_in(own_key, 6), dim), (parts,), jnp.float32, least / len(cuts), high / len(cuts))
        loudness = loudness * jnp.repeat(jnp.exp(steps), shape[dim] // parts).reshape((-1,) + (1,) * (len(shape) - 1 - dim))
    return loudness


def split_up(count, total, reach, skew):
    loads = [(1 << 20) // math.isqrt(standing ** skew) + 1 for standing in range(2, count + 1)]
    surplus, given = total - reach - (count - 1), [1] * (count - 1)
    while surplus > 0:
        candidates = [i for i in range(count - 1) if given[i] < reach]
        mass, left = sum([loads[i] for i in candidates]), surplus
        for i in candidates:
            more = min(reach - given[i], max(1, left * loads[i] // mass), surplus)
            given[i] = given[i] + more
            surplus = surplus - more
    return np.array([reach] + given)


def ragged(stream_key, amount, total, most, lean):
    if amount == 2:
        one = jax.random.randint(stream_key, (), max(1, total - most), min(most, total - 1) + 1)
        return jnp.stack([one, total - one])
    tallies = jnp.asarray(split_up(amount, total, most, lean), jnp.int32)
    twos = (amount - 1) // 2
    giver, taker = tallies[1:1 + 2 * twos:2], tallies[2:2 + 2 * twos:2]
    margin = jnp.minimum(giver - 1, most - taker)
    moved = jax.random.randint(jax.random.fold_in(stream_key, 1), (twos,), 0, 1 << 20) % (margin + 1)
    tallies = tallies.at[1:1 + 2 * twos:2].set(giver - moved).at[2:2 + 2 * twos:2].set(taker + moved)
    return tallies[jax.random.permutation(jax.random.fold_in(stream_key, 2), amount)]


def routed_block(own_key, own, number, rows, number_of, top, reach, lean):
    sequence = jax.random.permutation(own_key, number_of)
    crowded, common = portions_of(number_of, rows * top, reach, lean, True), portions_of(number_of, rows * top, reach, lean, False)
    places = jnp.arange(number_of)

    def named(sizes, turn):
        used = int((sizes > 0).sum())
        fixed = max(1, used // 4)
        shifted = fixed + (places - fixed + turn * (used - fixed)) % max(1, number_of - fixed)
        return jnp.zeros((number_of,), jnp.int32).at[sequence[jnp.where(places < fixed, places, shifted)]].set(jnp.asarray(sizes, jnp.int32))

    sizes = jnp.where(number % 4 == 0, named(crowded, number // 4), named(common, number - number // 4 - 1))
    mixed = jax.random.permutation(jax.random.fold_in(own, 3), number_of)
    giver, receiver = mixed[0:number_of // 2 * 2:2], mixed[1:number_of // 2 * 2:2]
    slack = jnp.minimum(sizes[giver] - 1, reach - sizes[receiver]) // 2
    slack = jnp.where((giver == sequence[0]) | (receiver == sequence[0]) | (sizes[receiver] == 0), 0, jnp.maximum(slack, 0))
    shifted = jax.random.randint(jax.random.fold_in(own, 4), (number_of // 2,), 0, 1 << 20) % (slack + 1)
    sizes = sizes.at[giver].add(-shifted).at[receiver].add(shifted)
    labels = jnp.searchsorted(jnp.cumsum(sizes), jnp.arange(rows * top), side="right").astype(jnp.int32)
    listing = labels.reshape(top, rows).T
    listing = listing[jax.random.permutation(jax.random.fold_in(own, 1), rows)]
    turn = jax.random.randint(jax.random.fold_in(own, 2), (rows, 1), 0, top)
    return jnp.take_along_axis(listing, (jnp.arange(top)[None, :] + turn) % top, axis=1)


def portions_of(count, total, limit, slope, full):
    weights = [(1 << 20) // math.isqrt(rank ** slope) + 1 for rank in range(1, count + 1)]
    largest = limit if full else min(limit, max(-(-total // count), total * weights[0] // sum(weights)))
    least = 1 if total - largest >= count - 1 else 0
    given, rest = [largest] + [least] * (count - 1), total - largest - least * (count - 1)
    while rest > 0:
        candidates = [i for i in range(1, count) if given[i] < largest] or [i for i in range(1, count) if given[i] < limit]
        pool, budget = sum([weights[i] for i in candidates]), rest
        for i in candidates:
            more = min(limit - given[i], max(1, budget * weights[i] // pool), rest)
            given[i] = given[i] + more
            rest = rest - more
    return np.array(given)


def centred(own_key, dims, width, reach, shards=(), kind=jnp.bfloat16):
    loudness = steps_of(own_key, dims, shards, -0.22, 0.18) if shards else 1.0
    values = jax.random.normal(own_key, dims, jnp.float32) * width * loudness
    return jnp.minimum(jnp.maximum(values, -reach), reach).astype(kind)


def setup_inputs(seed: int = 0) -> dict:
    seeds = jax.random.split(jax.random.key(seed), 10)
    patches = draw_patches(jax.random.fold_in(seeds[9], 71), 0)
    send_counts = draw_send_counts(jax.random.fold_in(seeds[9], 71), 0)
    window_ids = jax.vmap(lambda own: jnp.searchsorted(jnp.cumsum(ragged(own, 3, WIN, 40, 1)), jnp.arange(WIN), side="right"))(jax.random.split(seeds[2], (ROWS // WIN))).reshape((ROWS // WIN, WIN)).astype(jnp.int32)
    token_shard_keys = jax.random.split(jax.random.fold_in(seeds[3], 1), (N_DP * TOK) // TOK)
    token_shard_turns = jax.random.permutation(jax.random.fold_in(seeds[3], 3), (N_DP * TOK) // TOK)
    token_shard = jax.vmap(lambda own, number: routed_block(jax.random.fold_in(seeds[3], 2), own, number, TOK, N_DP, 1, TOKEN_CAP, 2))(token_shard_keys, token_shard_turns).reshape((N_DP * TOK, 1))
    first_gain = jnp.clip(1.0 + 0.15 * jax.random.normal(seeds[4], (D,), jnp.float32), 0.25, 1.75)
    qkv_weight = draw_qkv_weight(jax.random.fold_in(seeds[9], 71), 0)
    out_weight = centred(seeds[6], (D, D), D ** -0.5, 0.15625, ((1, 8),))
    merge_gain = jnp.clip(1.0 + 0.15 * jax.random.normal(seeds[7], (D,), jnp.float32), 0.25, 1.75)
    cotangent = centred(seeds[8], (N_DP * LM_DEV, 4, D), 0.05, 0.29882812, ((0, 64), (2, 8)))
    return dict(patches=patches, send_counts=send_counts, window_ids=window_ids, token_shard=token_shard, first_gain=first_gain, qkv_weight=qkv_weight, out_weight=out_weight, merge_gain=merge_gain, cotangent=cotangent)


EPS = 1e-06

def locate(counts, length):
    ends_at = jnp.cumsum(counts).astype(jnp.int32)
    starts = (ends_at - counts).astype(jnp.int32)
    position = jnp.arange(length, dtype=jnp.int32)
    source = lax.optimization_barrier(jnp.sum((ends_at[None, :] <= position[:, None]).astype(jnp.int32), axis=1)).astype(jnp.int32)
    source = jnp.minimum(source, counts.shape[0] - 1).astype(jnp.int32)
    offset = (position - jnp.take(starts, source)).astype(jnp.int32)
    filled = position < ends_at[-1]
    return (source, offset, filled)

def token_slots(token_shard, owners, tokens):
    target = token_shard[:, 0].reshape(owners, tokens).astype(jnp.int32)
    onehot = (target[:, :, None] == jnp.arange(owners, dtype=jnp.int32)[None, None, :]).astype(jnp.int32)
    earlier = (jnp.cumsum(onehot, axis=1) - onehot).astype(jnp.int32)
    order_in = lax.optimization_barrier(jnp.sum(earlier * onehot, axis=2)).astype(jnp.int32)
    counts = lax.optimization_barrier(jnp.sum(onehot, axis=1)).astype(jnp.int32)
    offsets = (jnp.cumsum(counts, axis=0) - counts).astype(jnp.int32)
    return (target, order_in, counts, offsets)

def widened(values):
    return lax.optimization_barrier(values).astype(jnp.float32)

def attend(packed, windows, scaling):
    queries = packed[:, :, :, 0].astype(jnp.float32)
    key_rows = packed[:, :, :, 1].astype(jnp.float32)
    values = packed[:, :, :, 2].astype(jnp.float32)
    scores = jnp.einsum('tqhe,tkhe->thqk', queries, key_rows) * scaling
    same_win = (windows[:, :, None] == windows[:, None, :])[:, None, :, :]
    scores = jnp.where(same_win, scores, -jnp.inf)
    highest = lax.optimization_barrier(jnp.max(scores, axis=3, keepdims=True))
    raised = jnp.exp(scores - highest)
    weights = raised / lax.optimization_barrier(jnp.sum(raised, axis=3, keepdims=True))
    rounded = weights.astype(jnp.bfloat16)
    output = jnp.einsum('thqk,tkhe->tqhe', widened(rounded), values).astype(jnp.bfloat16)
    return (output, weights, rounded)

def attend_back(grad_attn, packed, weights, rounded, scaling):
    queries = packed[:, :, :, 0].astype(jnp.float32)
    key_rows = packed[:, :, :, 1].astype(jnp.float32)
    values = packed[:, :, :, 2].astype(jnp.float32)
    upstream = grad_attn.astype(jnp.float32)
    dprobs = jnp.einsum('tqhe,tkhe->thqk', upstream, values)
    dvalues = jnp.einsum('thqk,tqhe->tkhe', widened(rounded), upstream).astype(jnp.bfloat16)
    row_dot = lax.optimization_barrier(jnp.sum(weights * dprobs, axis=3, keepdims=True))
    dscores = widened((weights * (dprobs - row_dot)).astype(jnp.bfloat16))
    dqueries = (jnp.einsum('thqk,tkhe->tqhe', dscores, key_rows) * scaling).astype(jnp.bfloat16)
    dkey_rows = (jnp.einsum('thqk,tqhe->tkhe', dscores, queries) * scaling).astype(jnp.bfloat16)
    return jnp.stack([dqueries, dkey_rows, dvalues], axis=3)

def reference(patches, send_counts, window_ids, token_shard, first_gain, qkv_weight, out_weight, merge_gain, cotangent):
    source_start = (jnp.cumsum(send_counts, axis=1) - send_counts).astype(jnp.int32)

    def owner_rows(owner_id):
        column = jnp.take(send_counts, owner_id, axis=1)
        source, offset, filled = locate(column, ROWS_OWN)
        first_row = jnp.take(jnp.take(source_start, owner_id, axis=1), source)
        return (source * ROWS_SRC + first_row + offset).astype(jnp.int32)
    gathered_index = jax.vmap(owner_rows)(jnp.arange(N_DP, dtype=jnp.int32)).reshape(-1)
    rows_in = jnp.take(patches, gathered_index, axis=0)
    stream = rows_in.astype(jnp.float32)
    inv_first = lax.rsqrt(lax.optimization_barrier(jnp.mean(stream * stream, axis=1, keepdims=True)) + EPS)
    normed_in = (stream * inv_first * first_gain).astype(jnp.bfloat16)
    packed = jnp.dot(normed_in, qkv_weight, preferred_element_type=jnp.float32).astype(jnp.bfloat16)
    tile_count = ROWS // WIN
    packed = packed.reshape(tile_count, WIN, HEADS, 3, HD)
    scaling = 1.0 / math.sqrt(HD)
    attn_tiles, weights, rounded = attend(packed, window_ids, scaling)
    attn = attn_tiles.reshape(ROWS, D)
    residual = stream + jnp.dot(attn, out_weight, preferred_element_type=jnp.float32)
    inv_second = lax.rsqrt(lax.optimization_barrier(jnp.mean(residual * residual, axis=1, keepdims=True)) + EPS)
    normed = (residual * inv_second * merge_gain).astype(jnp.bfloat16)
    tokens = normed.reshape(N_DP * TOK, 4, D)
    target, order_in, counts, offsets = token_slots(token_shard, N_DP, TOK)
    slot_row = (target * LM_DEV + jnp.take_along_axis(offsets, target, axis=1) + order_in).reshape(-1).astype(jnp.int32)
    merged_tokens = jnp.zeros((N_DP * LM_DEV, 4, D), jnp.bfloat16).at[slot_row].set(tokens)
    dnormed = jnp.take(cotangent, slot_row, axis=0).reshape(ROWS, D)
    upstream = dnormed.astype(jnp.float32)
    gain_grad = lax.optimization_barrier(jnp.sum(upstream * residual * inv_second, axis=0))
    along_rows = lax.optimization_barrier(jnp.sum(merge_gain * upstream * residual, axis=1, keepdims=True))
    dresidual = (merge_gain * upstream * inv_second - residual * along_rows * inv_second ** 3 / D).astype(jnp.bfloat16)
    out_grad = jnp.dot(attn.T, dresidual, preferred_element_type=jnp.float32).astype(jnp.bfloat16)
    summed = jnp.zeros((ROWS, D), jnp.float32)
    for group_id in range(N_TENSOR):
        low_col = group_id * GROUP_FEAT
        partial_value = jnp.dot(dresidual[:, low_col:low_col + GROUP_FEAT], out_weight[:, low_col:low_col + GROUP_FEAT].T, preferred_element_type=jnp.float32)
        summed = summed + widened(partial_value.astype(jnp.bfloat16))
    attn_grad = summed.astype(jnp.bfloat16).reshape(tile_count, WIN, HEADS, HD)
    dpacked = attend_back(attn_grad, packed, weights, rounded, scaling).reshape(ROWS, 3 * D)
    qkv_grad = jnp.dot(normed_in.T, dpacked, preferred_element_type=jnp.float32).astype(jnp.bfloat16)
    return (merged_tokens, qkv_grad, out_grad, gain_grad)
```

```python
import functools
import math

import jax
import jax.numpy as jnp
from jax import lax
from jax.experimental import pallas as pl
from jax.experimental.pallas import tpu as pltpu
from jax.sharding import PartitionSpec as P

HD = 80
WIN = 64


EPS = 1e-06


def locate(counts, length):
    ends_at = jnp.cumsum(counts)
    starts = ends_at - counts
    position = jnp.arange(length, dtype=jnp.int32)
    source = jnp.sum((ends_at[None, :] <= position[:, None]).astype(jnp.int32), axis=1)
    source = jnp.minimum(source, counts.shape[0] - 1)
    offset = position - jnp.take(starts, source)
    filled = position < ends_at[-1]
    return (source, offset, filled)


def token_slots(token_shard, owners, tokens):
    target = token_shard[:, 0].reshape(owners, tokens)
    onehot = (target[:, :, None] == jnp.arange(owners, dtype=jnp.int32)[None, None, :]).astype(
        jnp.int32
    )
    earlier = jnp.cumsum(onehot, axis=1) - onehot
    order_in = jnp.sum(earlier * onehot, axis=2)
    counts = jnp.sum(onehot, axis=1)
    offsets = jnp.cumsum(counts, axis=0) - counts
    return (target, order_in, counts, offsets)


def attend(packed, windows, scaling):
    queries = packed[:, :, :, 0]
    key_rows = packed[:, :, :, 1]
    values = packed[:, :, :, 2]
    scores = (
        jnp.einsum("tqhe,tkhe->thqk", queries, key_rows, preferred_element_type=jnp.float32)
        * scaling
    )
    same_win = (windows[:, :, None] == windows[:, None, :])[:, None, :, :]
    scores = jnp.where(same_win, scores, -jnp.inf)
    highest = jnp.max(scores, axis=3, keepdims=True)
    raised = jnp.exp(scores - highest)
    weights = raised / jnp.sum(raised, axis=3, keepdims=True)
    rounded = weights.astype(jnp.bfloat16)
    output = jnp.einsum(
        "thqk,tkhe->tqhe", rounded, values, preferred_element_type=jnp.float32
    ).astype(jnp.bfloat16)
    return (output, weights, rounded)


def attend_back(grad_attn, packed, weights, rounded, scaling):
    queries = packed[:, :, :, 0]
    key_rows = packed[:, :, :, 1]
    values = packed[:, :, :, 2]
    dprobs = jnp.einsum("tqhe,tkhe->thqk", grad_attn, values, preferred_element_type=jnp.float32)
    dvalues = jnp.einsum(
        "thqk,tqhe->tkhe", rounded, grad_attn, preferred_element_type=jnp.float32
    ).astype(jnp.bfloat16)
    row_dot = jnp.sum(weights * dprobs, axis=3, keepdims=True)
    dscores = (weights * (dprobs - row_dot)).astype(jnp.bfloat16)
    dqueries = (
        jnp.einsum("thqk,tkhe->tqhe", dscores, key_rows, preferred_element_type=jnp.float32)
        * scaling
    ).astype(jnp.bfloat16)
    dkey_rows = (
        jnp.einsum("thqk,tqhe->tkhe", dscores, queries, preferred_element_type=jnp.float32)
        * scaling
    ).astype(jnp.bfloat16)
    return jnp.stack([dqueries, dkey_rows, dvalues], axis=3)


def ragged(buffers):
    return lax.all_to_all(buffers, "dp", split_axis=0, concat_axis=0, tiled=True)


def full_rows(shard_part):
    return lax.all_gather(shard_part, "tensor", axis=1, tiled=True)


def row_total(values):
    return lax.psum(values, "tensor")


MESH = pl.DeviceIdType.MESH


def reduce_kernel(
    nz,
    ny,
    lhs_ref,
    rhs_ref,
    gain_ref,
    qkv_ref,
    out_ref,
    gsum_ref,
    part,
    full,
    c_buf,
    n_buf,
    p_buf,
    zs_up,
    zs_dn,
    zr_up,
    zr_dn,
    y_ss,
    y_rs,
    z_ss,
    z_rs,
    g_ss,
    g_rs,
    f_ss,
    f_rs,
):
    half = nz // 2
    width, cols = lhs_ref.shape[1], rhs_ref.shape[1]
    per_row = cols // 128
    live = (width // 16) * per_row
    tiles = part.shape[0]
    per = tiles // (nz * ny)
    me = lax.axis_index("dp")
    z, y = me // ny, lax.rem(me, ny)

    def dev(zz, yy):
        return {"dp": lax.rem(zz + nz, nz) * ny + lax.rem(yy + ny, ny)}

    up_y, dn_y, up_z, dn_z = dev(z, y + 1), dev(z, y - 1), dev(z + 1, y), dev(z - 1, y)
    barrier = pltpu.get_barrier_semaphore()
    for peer in (up_y, dn_y, up_z, dn_z):
        pl.semaphore_signal(barrier, inc=1, device_id=peer, device_id_type=MESH)

    block = 128
    per_block = (block // 16) * per_row

    def products(b, carry):
        got = lax.dot_general(
            lhs_ref[:, pl.ds(pl.multiple_of(b * block, block), block)],
            rhs_ref[...],
            (((0,), (0,)), ((), ())),
            preferred_element_type=jnp.float32,
        ).astype(jnp.bfloat16)
        for i in range(block // 16):
            for c in range(per_row):
                part[b * per_block + i * per_row + c] = got[16 * i : 16 * i + 16, 128 * c : 128 * c + 128]
        return carry

    lax.fori_loop(0, width // block, products, 0)
    part[pl.ds(live, tiles - live)] = jnp.zeros((tiles - live, 16, 128), jnp.bfloat16)
    part[live] = gain_ref[...].astype(jnp.bfloat16)

    pl.semaphore_wait(barrier, 4)

    def spot(yy, d):
        return pl.ds((lax.rem(yy + ny, ny) * nz + d) * per, per)

    def copy(src, dst, ss, rs, peer):
        return pltpu.make_async_remote_copy(
            src_ref=src, dst_ref=dst, send_sem=ss, recv_sem=rs, device_id=peer, device_id_type=MESH
        )

    def c_copy(d, fwd):
        src = part.at[spot(y + 2, d)]
        return copy(src, c_buf.at[d], y_ss.at[0, d], y_rs.at[0, d], up_y if fwd else dn_y)

    def n_copy(d, fwd):
        src = part.at[spot(y - 1 if fwd else y + 1, d)]
        return copy(src, n_buf.at[d], y_ss.at[1, d], y_rs.at[1, d], dn_y if fwd else up_y)

    def p_copy(d, fwd):
        src = part.at[spot(y + 1 if fwd else y - 1, d)]
        return copy(src, p_buf.at[d], y_ss.at[2, d], y_rs.at[2, d], up_y if fwd else dn_y)

    def both(d, act):
        even = lax.rem(d, 2) == 0

        @pl.when(even)
        def _():
            act(True)

        @pl.when(jnp.logical_not(even))
        def _():
            act(False)

    def y_first(d):
        def act(fwd):
            c_copy(d, fwd).start()
            n_copy(d, fwd).start()

        both(d, act)

    def y_second(d):
        def act(fwd):
            c_copy(d, fwd).wait_recv()
            here = spot(y + 1 if fwd else y - 1, d)
            total = part[here].astype(jnp.float32) + c_buf[d].astype(jnp.float32)
            part[here] = total.astype(jnp.bfloat16)
            p_copy(d, fwd).start()

        both(d, act)

    def y_sum(d):
        n_copy(d, True).wait_recv()
        p_copy(d, True).wait_recv()
        return (
            part[spot(y, d)].astype(jnp.float32)
            + n_buf[d].astype(jnp.float32)
            + p_buf[d].astype(jnp.float32)
        )

    def up_dest(k):
        return lax.rem(z + half - k, nz)

    def dn_dest(k):
        return lax.rem(z + nz - half + k, nz)

    def group(k, act):
        act(up_dest(k))

        @pl.when(jnp.logical_and(k > 0, k < half))
        def _():
            act(dn_dest(k))

    def zu_copy(k):
        return copy(zs_up.at[k], zr_up.at[k], z_ss.at[0, k], z_rs.at[0, k], up_z)

    def zd_copy(k):
        return copy(zs_dn.at[k], zr_dn.at[k], z_ss.at[1, k], z_rs.at[1, k], dn_z)

    ahead_first, ahead_second = 3, 1

    def first_group(k, carry):
        group(k, y_first)
        return carry

    def second_group(k, carry):
        group(k, y_second)
        return carry

    lax.fori_loop(0, ahead_first, first_group, 0)
    lax.fori_loop(0, ahead_second, second_group, 0)

    def z_step(k, carry):
        @pl.when(k + ahead_first <= half)
        def _():
            group(k + ahead_first, y_first)

        @pl.when(k + ahead_second <= half)
        def _():
            group(k + ahead_second, y_second)

        @pl.when(k == 0)
        def _():
            zs_up[k] = y_sum(up_dest(k)).astype(jnp.bfloat16)
            zu_copy(k).start()

        @pl.when(k > 0)
        def _():
            total = y_sum(up_dest(k))
            zu_copy(k - 1).wait_recv()
            zs_up[k] = (total + zr_up[k - 1].astype(jnp.float32)).astype(jnp.bfloat16)
            zu_copy(k).start()
            total = y_sum(dn_dest(k))

            @pl.when(k > 1)
            def _():
                zd_copy(k - 1).wait_recv()
                zs_dn[k] = (total + zr_dn[k - 1].astype(jnp.float32)).astype(jnp.bfloat16)

            @pl.when(k == 1)
            def _():
                zs_dn[k] = total.astype(jnp.bfloat16)

            zd_copy(k).start()

        return carry

    lax.fori_loop(0, half, z_step, 0)
    total = y_sum(z)
    zu_copy(half - 1).wait_recv()
    zd_copy(half - 1).wait_recv()
    own = spot(y, z)
    full[own] = (
        total + zr_up[half - 1].astype(jnp.float32) + zr_dn[half - 1].astype(jnp.float32)
    ).astype(jnp.bfloat16)

    def gz_up(s):
        at = full.at[spot(y, lax.rem(z - s + nz, nz))]
        return copy(at, at, g_ss.at[0, s], g_rs.at[0, s], up_z)

    def gz_dn(s):
        at = full.at[spot(y, lax.rem(z + s, nz))]
        return copy(at, at, g_ss.at[1, s], g_rs.at[1, s], dn_z)

    def gz_up_in(s):
        at = full.at[spot(y, lax.rem(z - s - 1 + nz, nz))]
        return copy(at, at, g_ss.at[0, s], g_rs.at[0, s], up_z)

    def gz_dn_in(s):
        at = full.at[spot(y, lax.rem(z + s + 1, nz))]
        return copy(at, at, g_ss.at[1, s], g_rs.at[1, s], dn_z)

    def ya_copy(d, yy):
        at = full.at[spot(yy, d)]
        return copy(at, at, f_ss.at[0, d], f_rs.at[0, d], up_y)

    def yb_copy(d, yy):
        at = full.at[spot(yy, d)]
        return copy(at, at, f_ss.at[1, d], f_rs.at[1, d], dn_y)

    def yf_copy(d, fwd):
        at = full.at[spot(y - 1 if fwd else y + 1, d)]
        return copy(at, at, f_ss.at[2, d], f_rs.at[2, d], up_y if fwd else dn_y)

    def spread(d):
        ya_copy(d, y).start()
        yb_copy(d, y).start()

    def onward(d):
        def act(fwd):
            if fwd:
                ya_copy(d, y - 1).wait_recv()
            else:
                yb_copy(d, y + 1).wait_recv()
            yf_copy(d, fwd).start()

        both(d, act)

    def g_step(s, carry):
        @pl.when(s > 0)
        def _():
            gz_up_in(s - 1).wait_recv()

        gz_up(s).start()

        @pl.when(jnp.logical_and(s > 0, s < half))
        def _():
            gz_dn_in(s - 1).wait_recv()

        @pl.when(s < half - 1)
        def _():
            gz_dn(s).start()

        spread(lax.rem(z - s + nz, nz))

        @pl.when(s > 0)
        def _():
            spread(lax.rem(z + s, nz))

        @pl.when(s > 1)
        def _():
            onward(lax.rem(z - s + 1 + nz, nz))
            onward(lax.rem(z + s - 1, nz))

        @pl.when(s == 1)
        def _():
            onward(z)

        return carry

    lax.fori_loop(0, half, g_step, 0)
    gz_up_in(half - 1).wait_recv()
    spread(lax.rem(z + half, nz))
    onward(lax.rem(z - half + 1 + nz, nz))
    onward(lax.rem(z + half - 1, nz))
    onward(lax.rem(z + half, nz))

    def arrivals(d, carry):
        def act(fwd):
            if fwd:
                yb_copy(d, y + 1).wait_recv()
            else:
                ya_copy(d, y - 1).wait_recv()
            at = full.at[spot(y + 2, d)]
            copy(at, at, f_ss.at[2, d], f_rs.at[2, d], up_y).wait_recv()

        both(d, act)
        return carry

    lax.fori_loop(0, nz, arrivals, 0)

    def unpack(r, carry):
        rows = pl.ds(pl.multiple_of(r * 16, 16), 16)
        for c in range(3):
            qkv_ref[rows, 128 * c : 128 * c + 128] = full[r * per_row + c]
        mixed = full[r * per_row + 3]
        qkv_ref[rows, 384:480] = mixed[:, :96]
        out_ref[rows, 128:160] = mixed[:, 96:]
        out_ref[rows, 0:128] = full[r * per_row + 4]
        return carry

    lax.fori_loop(0, width // 16, unpack, 0)
    gsum_ref[...] = full[live].astype(jnp.float32)

    def drain_y(d, carry):
        for j in range(3):
            copy(c_buf.at[d], c_buf.at[d], y_ss.at[j, d], y_rs.at[j, d], up_y).wait_send()
            copy(c_buf.at[d], c_buf.at[d], f_ss.at[j, d], f_rs.at[j, d], up_y).wait_send()
        return carry

    lax.fori_loop(0, nz, drain_y, 0)

    def drain_z(k, carry):
        zu_copy(k).wait_send()
        gz_up(k).wait_send()

        @pl.when(k > 0)
        def _():
            zd_copy(k).wait_send()

        @pl.when(k < half - 1)
        def _():
            gz_dn(k).wait_send()

        return carry

    lax.fori_loop(0, half, drain_z, 0)


def reduce_gradients(nz, ny, lhs, rhs, gain):
    width, cols = lhs.shape[1], rhs.shape[1]
    live = (width // 16) * (cols // 128)
    per = -(-(live + 1) // (nz * ny))
    half = nz // 2
    bf16 = jnp.bfloat16
    vmem = pl.BlockSpec(memory_space=pltpu.VMEM)
    sems = pltpu.SemaphoreType.DMA
    return pl.pallas_call(
        functools.partial(reduce_kernel, nz, ny),
        out_shape=(
            jax.ShapeDtypeStruct((width, 480), bf16),
            jax.ShapeDtypeStruct((width, 160), bf16),
            jax.ShapeDtypeStruct((16, 128), jnp.float32),
        ),
        in_specs=[vmem] * 3,
        out_specs=(vmem,) * 3,
        scratch_shapes=[
            pltpu.VMEM((per * nz * ny, 16, 128), bf16),
            pltpu.VMEM((per * nz * ny, 16, 128), bf16),
            pltpu.VMEM((nz, per, 16, 128), bf16),
            pltpu.VMEM((nz, per, 16, 128), bf16),
            pltpu.VMEM((nz, per, 16, 128), bf16),
            pltpu.VMEM((half, per, 16, 128), bf16),
            pltpu.VMEM((half, per, 16, 128), bf16),
            pltpu.VMEM((half, per, 16, 128), bf16),
            pltpu.VMEM((half, per, 16, 128), bf16),
            sems((3, nz)),
            sems((3, nz)),
            sems((2, half)),
            sems((2, half)),
            sems((2, half)),
            sems((2, half)),
            sems((3, nz)),
            sems((3, nz)),
        ],
        compiler_params=pltpu.CompilerParams(
            collective_id=0, has_side_effects=True, vmem_limit_bytes=48 * 1024 * 1024
        ),
        name="reduce_gradients",
    )(lhs, rhs, gain)


def body(
    patches,
    send_counts,
    window_ids,
    token_shard,
    first_gain,
    qkv_weight,
    out_weight,
    merge_gain,
    cotangent,
):
    devices = lax.axis_size("dp")
    device = lax.axis_index("dp")
    rows_src, features = patches.shape
    rows_own = rows_src // 2
    slot_cap = rows_src // devices
    tokens = rows_own // 4
    lm_slots = cotangent.shape[0]
    token_cap = lm_slots // devices
    model_width = first_gain.shape[0]
    scaling = 1.0 / math.sqrt(HD)
    source_start = jnp.cumsum(send_counts, axis=1) - send_counts
    own_start = lax.dynamic_index_in_dim(source_start, device, 0, keepdims=False)
    pick_rows = jnp.minimum(
        own_start[:, None] + jnp.arange(slot_cap, dtype=jnp.int32)[None, :], rows_src - 1
    )
    outgoing = jnp.take(patches, pick_rows.reshape(-1), axis=0).reshape(devices, slot_cap, features)
    target, order_in, counts, offsets = token_slots(token_shard, devices, tokens)
    lm_counts = lax.dynamic_index_in_dim(counts, device, 1, keepdims=False)
    lm_offsets = lax.dynamic_index_in_dim(offsets, device, 1, keepdims=False)
    back_picks = jnp.minimum(
        lm_offsets[:, None] + jnp.arange(token_cap, dtype=jnp.int32)[None, :], lm_slots - 1
    )
    flat_cot = cotangent.reshape(lm_slots, 4 * features)
    returning = jnp.take(flat_cot, back_picks.reshape(-1), axis=0).reshape(
        devices, token_cap, 4 * features
    )
    arrived = ragged(outgoing)
    owner_counts = lax.dynamic_index_in_dim(send_counts, device, 1, keepdims=False)
    source, offset, filled_own = locate(owner_counts, rows_own)
    rows_in = jnp.take(
        arrived.reshape(devices * slot_cap, features), source * slot_cap + offset, axis=0
    )
    whole_rows = full_rows(rows_in)
    stream_all = whole_rows.astype(jnp.float32)
    inv_first = lax.rsqrt(jnp.mean(stream_all * stream_all, axis=1, keepdims=True) + EPS)
    normed_in = (stream_all * inv_first * first_gain).astype(jnp.bfloat16)
    packed = jnp.dot(normed_in, qkv_weight, preferred_element_type=jnp.float32).astype(jnp.bfloat16)
    heads_here = packed.shape[1] // (3 * HD)
    packed = packed.reshape(rows_own // WIN, WIN, heads_here, 3, HD)
    attn_tiles, weights, rounded = attend(packed, window_ids, scaling)
    attn_part = attn_tiles.reshape(rows_own, heads_here * HD)
    attn_all = full_rows(attn_part)
    residual = rows_in.astype(jnp.float32) + jnp.dot(
        attn_all, out_weight, preferred_element_type=jnp.float32
    )
    inv_second = lax.rsqrt(row_total(jnp.sum(residual * residual, axis=1)) / model_width + EPS)[
        :, None
    ]
    normed = (residual * inv_second * merge_gain).astype(jnp.bfloat16)
    own_target = lax.dynamic_index_in_dim(target, device, 0, keepdims=False)
    own_order = lax.dynamic_index_in_dim(order_in, device, 0, keepdims=False)
    slot_index = own_target * token_cap + own_order
    sending = (
        jnp.zeros((devices * token_cap, 4 * features), jnp.bfloat16)
        .at[slot_index]
        .set(normed.reshape(tokens, 4 * features))
    )
    landed = ragged(sending.reshape(devices, token_cap, 4 * features)).reshape(
        devices * token_cap, 4 * features
    )
    source_lm, offset_lm, filled_lm = locate(lm_counts, lm_slots)
    merged_rows = jnp.take(landed, source_lm * token_cap + offset_lm, axis=0)
    merged_tokens = jnp.where(filled_lm[:, None], merged_rows, jnp.zeros_like(merged_rows)).reshape(
        lm_slots, 4, features
    )
    came_back = ragged(returning).reshape(devices * token_cap, 4 * features)
    upstream_bf = jnp.take(came_back, slot_index, axis=0).reshape(rows_own, features)
    upstream = upstream_bf.astype(jnp.float32)
    gain_part = jnp.sum(upstream * residual * inv_second, axis=0)
    along_rows = row_total(jnp.sum(merge_gain * upstream * residual, axis=1))[:, None]
    dresidual = (
        merge_gain * upstream * inv_second - residual * along_rows * inv_second**3 / model_width
    ).astype(jnp.bfloat16)
    spread = lax.dot_general(
        dresidual, out_weight, (((1,), (1,)), ((), ())), preferred_element_type=jnp.float32
    )
    attn_grad = lax.psum_scatter(
        spread.astype(jnp.bfloat16), "tensor", scatter_dimension=1, tiled=True
    )
    dpacked = attend_back(
        attn_grad.reshape(rows_own // WIN, WIN, heads_here, HD), packed, weights, rounded, scaling
    )
    dpacked = dpacked.reshape(rows_own, 3 * heads_here * HD)
    lhs = jnp.concatenate([normed_in, attn_all], axis=0)
    swapped = jnp.concatenate([dresidual[:, 128:], dresidual[:, :128]], axis=1)
    rhs = jnp.concatenate(
        [
            jnp.pad(dpacked, ((0, 0), (0, features))),
            jnp.pad(swapped, ((0, 0), (dpacked.shape[1], 0))),
        ],
        axis=0,
    )
    gain_tile = jnp.pad(gain_part, (0, 16 * 128 - features)).reshape(16, 128)
    qkv_grad, out_grad, gain_sum = reduce_gradients(devices // 4, 4, lhs, rhs, gain_tile)
    gain_grad = gain_sum.reshape(-1)[:features]
    return (merged_tokens, qkv_grad, out_grad, gain_grad)


def solution(mesh):
    placed = (
        P("dp", "tensor"),
        P(),
        P("dp", None),
        P(),
        P(),
        P(None, "tensor"),
        P(None, "tensor"),
        P("tensor"),
        P("dp", None, "tensor"),
    )
    return jax.shard_map(
        body,
        mesh=mesh,
        in_specs=placed,
        out_specs=(P("dp", None, "tensor"), P(None, "tensor"), P(None, "tensor"), P("tensor")),
        check_vma=False,
    )
```

```python
import functools
import math

import jax
import jax.numpy as jnp
from jax import lax
from jax.experimental import pallas as pl
from jax.experimental.pallas import tpu as pltpu
from jax.sharding import PartitionSpec as P

HD = 80
WIN = 64
EPS = 1e-06
NY = 4
MESH = pl.DeviceIdType.MESH


def copy(src, dst, ss, rs, peer):
    return pltpu.make_async_remote_copy(
        src_ref=src, dst_ref=dst, send_sem=ss, recv_sem=rs, device_id=peer, device_id_type=MESH
    )


def iota(shape, dim):
    return lax.broadcasted_iota(jnp.int32, shape, dim)


def pick(cond):
    return jnp.where(cond, 1.0, 0.0).astype(jnp.bfloat16)


def to_row(col):
    n = col.shape[0]
    return jnp.sum(jnp.where(iota((n, n), 0) == iota((n, n), 1), col, 0.0), axis=0, keepdims=True)


def to_col(row):
    n = row.shape[1]
    return jnp.sum(jnp.where(iota((n, n), 0) == iota((n, n), 1), row, 0.0), axis=1, keepdims=True)


def dot(a, b, ca=1, cb=0):
    return lax.dot_general(a, b, (((ca,), (cb,)), ((), ())), preferred_element_type=jnp.float32)


def sum_chunks(
    nz,
    ny,
    me,
    z,
    y,
    dev,
    meanwhile,
    lhs_ref,
    rhs_ref,
    gain_ref,
    qkv_ref,
    out_ref,
    gsum_ref,
    part,
    full,
    c_buf,
    n_buf,
    p_buf,
    zs_up,
    zs_dn,
    zr_up,
    zr_dn,
    y_ss,
    y_rs,
    z_ss,
    z_rs,
    g_ss,
    g_rs,
    f_ss,
    f_rs,
):
    up_y, dn_y, up_z, dn_z = dev(z, y + 1), dev(z, y - 1), dev(z + 1, y), dev(z - 1, y)
    half = nz // 2
    width, cols = lhs_ref.shape[0], rhs_ref.shape[0]
    per_row = cols // 128
    live = (width // 16) * per_row
    tiles = part.shape[0]
    per = tiles // (nz * ny)
    block = 160
    per_block = (block // 16) * per_row

    def products(b, carry):
        got = lax.dot_general(
            lhs_ref[pl.ds(pl.multiple_of(b * block, block), block), :],
            rhs_ref[...],
            (((1,), (1,)), ((), ())),
            preferred_element_type=jnp.float32,
        ).astype(jnp.bfloat16)
        for i in range(block // 16):
            for c in range(per_row):
                part[b * per_block + i * per_row + c] = got[16 * i : 16 * i + 16, 128 * c : 128 * c + 128]
        return carry

    lax.fori_loop(0, width // block, products, 0)
    part[pl.ds(live, tiles - live)] = jnp.zeros((tiles - live, 16, 128), jnp.bfloat16)
    part[live] = gain_ref[...].astype(jnp.bfloat16)

    def spot(yy, d):
        return pl.ds((lax.rem(yy + ny, ny) * nz + d) * per, per)

    def c_copy(d, fwd):
        src = part.at[spot(y + 2, d)]
        return copy(src, c_buf.at[d], y_ss.at[0, d], y_rs.at[0, d], up_y if fwd else dn_y)

    def n_copy(d, fwd):
        src = part.at[spot(y - 1 if fwd else y + 1, d)]
        return copy(src, n_buf.at[d], y_ss.at[1, d], y_rs.at[1, d], dn_y if fwd else up_y)

    def p_copy(d, fwd):
        src = part.at[spot(y + 1 if fwd else y - 1, d)]
        return copy(src, p_buf.at[d], y_ss.at[2, d], y_rs.at[2, d], up_y if fwd else dn_y)

    def both(d, act):
        even = lax.rem(d, 2) == 0

        @pl.when(even)
        def _():
            act(True)

        @pl.when(jnp.logical_not(even))
        def _():
            act(False)

    def y_first(d):
        def act(fwd):
            c_copy(d, fwd).start()
            n_copy(d, fwd).start()

        both(d, act)

    def y_second(d):
        def act(fwd):
            c_copy(d, fwd).wait_recv()
            here = spot(y + 1 if fwd else y - 1, d)
            total = part[here].astype(jnp.float32) + c_buf[d].astype(jnp.float32)
            part[here] = total.astype(jnp.bfloat16)
            p_copy(d, fwd).start()

        both(d, act)

    def y_sum(d):
        n_copy(d, True).wait_recv()
        p_copy(d, True).wait_recv()
        return (
            part[spot(y, d)].astype(jnp.float32)
            + n_buf[d].astype(jnp.float32)
            + p_buf[d].astype(jnp.float32)
        )

    def up_dest(k):
        return lax.rem(z + half - k, nz)

    def dn_dest(k):
        return lax.rem(z + nz - half + k, nz)

    def group(k, act):
        act(up_dest(k))

        @pl.when(jnp.logical_and(k > 0, k < half))
        def _():
            act(dn_dest(k))

    def zu_copy(k):
        return copy(zs_up.at[k], zr_up.at[k], z_ss.at[0, k], z_rs.at[0, k], up_z)

    def zd_copy(k):
        return copy(zs_dn.at[k], zr_dn.at[k], z_ss.at[1, k], z_rs.at[1, k], dn_z)

    ahead_first, ahead_second = 3, 1

    def first_group(k, carry):
        group(k, y_first)
        return carry

    def second_group(k, carry):
        group(k, y_second)
        return carry

    lax.fori_loop(0, ahead_first, first_group, 0)
    lax.fori_loop(0, ahead_second, second_group, 0)

    def z_step(k, carry):
        @pl.when(k + ahead_first <= half)
        def _():
            group(k + ahead_first, y_first)

        @pl.when(k + ahead_second <= half)
        def _():
            group(k + ahead_second, y_second)

        @pl.when(k == 0)
        def _():
            zs_up[k] = y_sum(up_dest(k)).astype(jnp.bfloat16)
            zu_copy(k).start()

        @pl.when(k > 0)
        def _():
            total = y_sum(up_dest(k))
            zu_copy(k - 1).wait_recv()
            zs_up[k] = (total + zr_up[k - 1].astype(jnp.float32)).astype(jnp.bfloat16)
            zu_copy(k).start()
            total = y_sum(dn_dest(k))

            @pl.when(k > 1)
            def _():
                zd_copy(k - 1).wait_recv()
                zs_dn[k] = (total + zr_dn[k - 1].astype(jnp.float32)).astype(jnp.bfloat16)

            @pl.when(k == 1)
            def _():
                zs_dn[k] = total.astype(jnp.bfloat16)

            zd_copy(k).start()

        return carry

    lax.fori_loop(0, half, z_step, 0)
    total = y_sum(z)
    zu_copy(half - 1).wait_recv()
    zd_copy(half - 1).wait_recv()
    own = spot(y, z)
    full[own] = (
        total + zr_up[half - 1].astype(jnp.float32) + zr_dn[half - 1].astype(jnp.float32)
    ).astype(jnp.bfloat16)

    def gz_up(s):
        at = full.at[spot(y, lax.rem(z - s + nz, nz))]
        return copy(at, at, g_ss.at[0, s], g_rs.at[0, s], up_z)

    def gz_dn(s):
        at = full.at[spot(y, lax.rem(z + s, nz))]
        return copy(at, at, g_ss.at[1, s], g_rs.at[1, s], dn_z)

    def gz_up_in(s):
        at = full.at[spot(y, lax.rem(z - s - 1 + nz, nz))]
        return copy(at, at, g_ss.at[0, s], g_rs.at[0, s], up_z)

    def gz_dn_in(s):
        at = full.at[spot(y, lax.rem(z + s + 1, nz))]
        return copy(at, at, g_ss.at[1, s], g_rs.at[1, s], dn_z)

    def ya_copy(d, yy):
        at = full.at[spot(yy, d)]
        return copy(at, at, f_ss.at[0, d], f_rs.at[0, d], up_y)

    def yb_copy(d, yy):
        at = full.at[spot(yy, d)]
        return copy(at, at, f_ss.at[1, d], f_rs.at[1, d], dn_y)

    def yf_copy(d, fwd):
        at = full.at[spot(y - 1 if fwd else y + 1, d)]
        return copy(at, at, f_ss.at[2, d], f_rs.at[2, d], up_y if fwd else dn_y)

    def spread(d):
        ya_copy(d, y).start()
        yb_copy(d, y).start()

    def onward(d):
        def act(fwd):
            if fwd:
                ya_copy(d, y - 1).wait_recv()
            else:
                yb_copy(d, y + 1).wait_recv()
            yf_copy(d, fwd).start()

        both(d, act)

    def g_step(s, carry):
        @pl.when(s > 0)
        def _():
            gz_up_in(s - 1).wait_recv()

        gz_up(s).start()

        @pl.when(jnp.logical_and(s > 0, s < half))
        def _():
            gz_dn_in(s - 1).wait_recv()

        @pl.when(s < half - 1)
        def _():
            gz_dn(s).start()

        spread(lax.rem(z - s + nz, nz))

        @pl.when(s > 0)
        def _():
            spread(lax.rem(z + s, nz))

        @pl.when(s > 1)
        def _():
            onward(lax.rem(z - s + 1 + nz, nz))
            onward(lax.rem(z + s - 1, nz))

        @pl.when(s == 1)
        def _():
            onward(z)

        return carry

    lax.fori_loop(0, half, g_step, 0)
    gz_up_in(half - 1).wait_recv()
    spread(lax.rem(z + half, nz))
    onward(lax.rem(z - half + 1 + nz, nz))
    onward(lax.rem(z + half - 1, nz))
    onward(lax.rem(z + half, nz))

    def arrivals(d, carry):
        def act(fwd):
            if fwd:
                yb_copy(d, y + 1).wait_recv()
            else:
                ya_copy(d, y - 1).wait_recv()
            at = full.at[spot(y + 2, d)]
            copy(at, at, f_ss.at[2, d], f_rs.at[2, d], up_y).wait_recv()

        both(d, act)
        return carry

    meanwhile()
    lax.fori_loop(0, nz, arrivals, 0)

    def unpack(r, carry):
        rows = pl.ds(pl.multiple_of(r * 16, 16), 16)
        for c in range(3):
            qkv_ref[rows, 128 * c : 128 * c + 128] = full[r * per_row + c]
        mixed = full[r * per_row + 3]
        qkv_ref[rows, 384:480] = mixed[:, :96]
        out_ref[rows, 128:160] = mixed[:, 96:]
        out_ref[rows, 0:128] = full[r * per_row + 4]
        return carry

    lax.fori_loop(0, width // 16, unpack, 0)
    gsum_ref[...] = full[live].astype(jnp.float32)

    def drain_y(d, carry):
        for j in range(3):
            copy(c_buf.at[d], c_buf.at[d], y_ss.at[j, d], y_rs.at[j, d], up_y).wait_send()
            copy(c_buf.at[d], c_buf.at[d], f_ss.at[j, d], f_rs.at[j, d], up_y).wait_send()
        return carry

    lax.fori_loop(0, nz, drain_y, 0)

    def drain_z(k, carry):
        zu_copy(k).wait_send()
        gz_up(k).wait_send()

        @pl.when(k > 0)
        def _():
            zd_copy(k).wait_send()

        @pl.when(k < half - 1)
        def _():
            gz_dn(k).wait_send()

        return carry

    lax.fori_loop(0, half, drain_z, 0)


def layer_kernel(
    nz,
    ny,
    patches_ref,
    counts_ref,
    ids_ref,
    tok_ref,
    gain1_ref,
    wqkv_ref,
    wout_ref,
    gain2_ref,
    cot_ref,
    merged_ref,
    qkv_ref,
    out_ref,
    gsum_ref,
    row_out,
    row_mid,
    row_in,
    cot_out,
    cot_mid,
    cot_in,
    tok_out,
    tok_mid,
    tok_in,
    x_all,
    attn_all,
    stat_all,
    spread,
    grad_in,
    wqkv_t,
    wout_t,
    gain_col,
    lhs,
    rhs,
    gain_tile,
    hop_ss,
    hop_rs,
    far_ss,
    far_rs,
    t_ss,
    t_rs,
    *reduce_refs,
):
    bf16, f32 = jnp.bfloat16, jnp.float32
    dp = nz * ny
    nt = lax.axis_size("tensor")
    me = lax.axis_index("dp")
    rank = lax.axis_index("tensor")
    z, y = me // ny, lax.rem(me, ny)
    rows_src, features = patches_ref.shape
    rows_own = x_all.shape[1]
    width = x_all.shape[0]
    slot_cap = rows_src // dp
    lm_rows = cot_ref.shape[0]
    token_rows = lm_rows // dp
    token_cap = token_rows // 4
    tokens = rows_own // 4
    heads = wqkv_ref.shape[1] // (3 * HD)
    scaling = 1.0 / math.sqrt(HD)
    log = lambda n: n.bit_length() - 1

    def dev(zz, yy):
        return {"dp": lax.rem(zz + nz, nz) * ny + lax.rem(yy + ny, ny)}

    def mate(i):
        return {"tensor": lax.rem(rank + i, nt)}

    barrier = pltpu.get_barrier_semaphore()
    for i in range(1, ny):
        pl.semaphore_signal(barrier, inc=1, device_id=dev(z, y + i), device_id_type=MESH)
    for i in range(1, nt):
        pl.semaphore_signal(barrier, inc=1, device_id=mate(i), device_id_type=MESH)
    for i in range(1, nz):
        pl.semaphore_signal(barrier, inc=1, device_id=dev(z + i, y), device_id_type=MESH)

    def owner_of(shape, dim, per):
        at = iota(shape, dim) >> log(per)
        return (at & (nz - 1)) * ny + (at >> log(nz))

    def hop(k, out, mid, i):
        to = lax.rem(y + i, ny)
        return copy(out.at[to], mid.at[y], hop_ss.at[k, i - 1], hop_rs.at[k, i - 1], dev(z, y + i))

    def far(k, mid, got, i):
        to = lax.rem(z + i, nz)
        return copy(
            mid.at[:, to], got.at[z], far_ss.at[k, i - 1], far_rs.at[k, i - 1], dev(z + i, y)
        )

    def first_hop(k, out, mid):
        for i in range(1, ny):
            hop(k, out, mid, i).start()
        mid[y] = out[y]

    def second_hop(k, out, mid, got):
        for i in range(1, ny):
            hop(k, out, mid, i).wait_recv()

        def send(i, carry):
            far(k, mid, got, i).start()
            return carry

        lax.fori_loop(1, nz, send, 0)
        got[z] = mid[:, z]

    def landed(k, mid, got):
        def take(i, carry):
            far(k, mid, got, i).wait_recv()
            return carry

        lax.fori_loop(1, nz, take, 0)

    n = rows_src
    own_row = counts_ref[pl.ds(me, 1), :].astype(f32)
    start = jnp.sum(
        jnp.where(iota((n, dp), 1) < owner_of((n, dp), 0, slot_cap), own_row, 0.0),
        axis=1,
        keepdims=True,
    ).astype(jnp.int32)
    slot = iota((n, 1), 0) & (slot_cap - 1)
    chosen = pick(iota((n, rows_src), 1) == jnp.minimum(start + slot, rows_src - 1))
    row_out[...] = dot(chosen, patches_ref[...]).reshape(row_out.shape).astype(bf16)

    pl.semaphore_wait(barrier, ny - 1 + nt - 1 + nz - 1)
    first_hop(0, row_out, row_mid)

    tok = tok_ref[...]
    lm_col = jnp.sum(jnp.where(tok == me, 1.0, 0.0), axis=1, keepdims=True)
    lm_row = to_row(lm_col)
    n = lm_rows
    start = jnp.sum(
        jnp.where(iota((n, dp), 1) < owner_of((n, dp), 0, token_rows), lm_row, 0.0),
        axis=1,
        keepdims=True,
    ).astype(jnp.int32)
    slot = (iota((n, 1), 0) & (token_rows - 1)) >> 2
    quarter = iota((n, 1), 0) & 3
    place = jnp.minimum(start + slot, lm_rows // 4 - 1) * 4 + quarter
    chosen = pick(iota((n, n), 1) == place)
    cot_out[...] = dot(chosen, cot_ref[...]).reshape(cot_out.shape).astype(bf16)

    second_hop(0, row_out, row_mid, row_in)
    first_hop(1, cot_out, cot_mid)

    n = rows_src
    sent_col = jnp.sum(
        jnp.where(iota((dp, dp), 1) == me, counts_ref[...].astype(f32), 0.0), axis=1, keepdims=True
    )
    sent_row = to_row(sent_col)
    source = iota((n, dp), 0) >> log(slot_cap)
    start = jnp.sum(jnp.where(iota((n, dp), 1) < source, sent_row, 0.0), axis=1, keepdims=True)
    count = jnp.sum(jnp.where(iota((n, dp), 1) == source, sent_row, 0.0), axis=1, keepdims=True)
    slot = iota((n, 1), 0) & (slot_cap - 1)
    where_to = jnp.where(slot < count.astype(jnp.int32), start.astype(jnp.int32) + slot, -1)
    placed = pick(iota((n, rows_own), 1) == where_to)

    wqkv_t[...] = wqkv_ref[...].T
    second_hop(1, cot_out, cot_mid, cot_in)

    landed(0, row_mid, row_in)
    own = pl.ds(pl.multiple_of(rank * features, 16), features)
    arrived = row_in[...].astype(f32).reshape(rows_src, features).astype(bf16)
    x_own = dot(arrived, placed, 0, 0)
    x_all[own, :] = x_own.astype(bf16)

    def gather(k, buf, i):
        return copy(buf.at[own, :], buf.at[own, :], t_ss.at[k, i - 1], t_rs.at[k, i - 1], mate(i))

    for i in range(1, nt):
        gather(0, x_all, i).start()

    wout_t[...] = wout_ref[...].T
    for b in range(width // 160):
        gain_col[160 * b : 160 * b + 160, :] = to_col(gain1_ref[:, 160 * b : 160 * b + 160])
    merge_gain = to_col(gain2_ref[...])
    ids_row = ids_ref[...].astype(f32)
    same = to_col(ids_row) == ids_row

    target = tok_ref[pl.ds(me, 1), :].astype(f32)
    target_col = to_col(target)
    before = iota((tokens, tokens), 0) < iota((tokens, tokens), 1)
    order = jnp.sum(
        jnp.where(jnp.logical_and(target_col == target, before), 1.0, 0.0), axis=0, keepdims=True
    )
    token_slot = to_col(target * token_rows + order * 4)
    of_row = iota((tokens, rows_own), 1) >> 2
    slot_row = jnp.sum(
        jnp.where(iota((tokens, rows_own), 0) == of_row, token_slot, 0.0), axis=0, keepdims=True
    ).astype(jnp.int32) + (iota((1, rows_own), 1) & 3)
    taken = pick(iota((lm_rows, rows_own), 0) == slot_row)
    sent_id = owner_of((lm_rows, rows_own), 0, token_rows) * token_rows + (
        iota((lm_rows, rows_own), 0) & (token_rows - 1)
    )
    given = pick(sent_id == slot_row)

    for i in range(1, nt):
        gather(0, x_all, i).wait_recv()
    x = x_all[...].astype(f32)
    inv_first = lax.rsqrt(jnp.sum(x * x, axis=0, keepdims=True) / width + EPS)
    normed_in = (x * inv_first * gain_col[...]).astype(bf16)
    lhs[:, 0:rows_own] = normed_in
    packed = dot(wqkv_t[...], normed_in).astype(bf16)

    kept = []
    for h in range(heads):
        q, k, v = (packed[(3 * h + s) * HD : (3 * h + s + 1) * HD] for s in range(3))
        scores = jnp.where(same, dot(k, q, 0, 0) * scaling, -jnp.inf)
        raised = jnp.exp(scores - jnp.max(scores, axis=0, keepdims=True))
        weights = raised / jnp.sum(raised, axis=0, keepdims=True)
        rounded = weights.astype(bf16)
        at = pl.ds(pl.multiple_of(rank * features + h * HD, 16), HD)
        attn_all[at, :] = dot(v, rounded).astype(bf16)
        kept.append((q, k, v, weights, rounded))

    for i in range(1, nt):
        gather(1, attn_all, i).start()
    landed(1, cot_mid, cot_in)
    returned = cot_in[...].astype(f32).reshape(lm_rows, features).astype(bf16)
    upstream = dot(returned, taken, 0, 0)
    for i in range(1, nt):
        gather(1, attn_all, i).wait_recv()

    attn = attn_all[...]
    lhs[:, rows_own : 2 * rows_own] = attn
    residual = x_own + dot(wout_t[...], attn)
    lifted = merge_gain * upstream
    sums = [
        jnp.sum(residual * residual, axis=0, keepdims=True),
        jnp.sum(lifted * residual, axis=0, keepdims=True),
    ]
    stat_all[rank] = jnp.concatenate(sums + [jnp.zeros((6, rows_own), f32)], axis=0)

    def stat(i):
        at = stat_all.at[rank]
        return copy(at, at, t_ss.at[2, i - 1], t_rs.at[2, i - 1], mate(i))

    for i in range(1, nt):
        stat(i).start()
    for i in range(1, nt):
        stat(i).wait_recv()
    stats = jnp.sum(stat_all[...], axis=0)
    inv_second = lax.rsqrt(stats[0:1] / width + EPS)
    along = stats[1:2]
    scaled = residual * inv_second
    dresidual = (
        lifted * inv_second - residual * (along * (inv_second * inv_second * inv_second) / width)
    ).astype(bf16)
    spread[...] = dot(wout_ref[...], dresidual).astype(bf16)

    def share(i):
        to = lax.rem(rank + i, nt)
        src = spread.at[pl.ds(pl.multiple_of(to * features, 16), features), :]
        return copy(src, grad_in.at[rank], t_ss.at[3, i - 1], t_rs.at[3, i - 1], mate(i))

    for i in range(1, nt):
        share(i).start()
    grad_in[rank] = spread[own, :]

    normed = (scaled * merge_gain).astype(bf16)
    tok_out[...] = dot(given, normed, 1, 1).reshape(tok_out.shape).astype(bf16)
    first_hop(2, tok_out, tok_mid)

    gains = jnp.sum(upstream * scaled, axis=1, keepdims=True)
    lane, sub = iota((features, 128), 1), iota((features, 128), 0)
    head = jnp.sum(jnp.where(lane == sub, gains, 0.0), axis=0, keepdims=True)
    tail = jnp.sum(jnp.where(lane + 128 == sub, gains, 0.0), axis=0, keepdims=True)
    gain_tile[...] = jnp.concatenate([head, tail, jnp.zeros((14, 128), f32)], axis=0)

    base = 3 * heads * HD
    rhs[0:base, rows_own : 2 * rows_own] = jnp.zeros((base, rows_own), bf16)
    rhs[base : base + features, 0:rows_own] = jnp.zeros((features, rows_own), bf16)
    rhs[base : base + features - 128, rows_own : 2 * rows_own] = dresidual[128:]
    rhs[base + features - 128 : base + features, rows_own : 2 * rows_own] = dresidual[:128]

    second_hop(2, tok_out, tok_mid, tok_in)
    for i in range(1, nt):
        share(i).wait_recv()
    total = grad_in[0].astype(f32)
    for r in range(1, nt):
        total = total + grad_in[r].astype(f32)
    attn_grad = total.astype(bf16)

    for h in range(heads):
        q, k, v, weights, rounded = kept[h]
        g = attn_grad[h * HD : (h + 1) * HD]
        dprobs = dot(v, g, 0, 0)
        row_dot = jnp.sum(weights * dprobs, axis=0, keepdims=True)
        dscores = (weights * (dprobs - row_dot)).astype(bf16)
        at = 3 * h * HD
        rhs[at : at + HD, 0:rows_own] = (dot(k, dscores) * scaling).astype(bf16)
        rhs[at + HD : at + 2 * HD, 0:rows_own] = (dot(q, dscores, 1, 1) * scaling).astype(bf16)
        rhs[at + 2 * HD : at + 3 * HD, 0:rows_own] = dot(g, rounded, 1, 1).astype(bf16)

    def place_tokens():
        landed(2, tok_mid, tok_in)
        n = lm_rows
        owner = iota((dp, n), 1) >> log(token_rows)
        start = jnp.sum(jnp.where(iota((dp, n), 0) < owner, lm_col, 0.0), axis=0, keepdims=True)
        count = jnp.sum(jnp.where(iota((dp, n), 0) == owner, lm_col, 0.0), axis=0, keepdims=True)
        slot = (iota((1, n), 1) & (token_rows - 1)) >> 2
        to = (start.astype(jnp.int32) + slot) * 4 + (iota((1, n), 1) & 3)
        to = jnp.where(slot < count.astype(jnp.int32), to, -1)
        put = pick(iota((n, n), 0) == to)
        got = tok_in[...].astype(f32).reshape(n, features).astype(bf16)
        merged_ref[...] = dot(put, got).astype(bf16)

    sum_chunks(
        nz,
        ny,
        me,
        z,
        y,
        dev,
        place_tokens,
        lhs,
        rhs,
        gain_tile,
        qkv_ref,
        out_ref,
        gsum_ref,
        *reduce_refs,
    )

    for k, (out, mid, got) in enumerate(
        ((row_out, row_mid, row_in), (cot_out, cot_mid, cot_in), (tok_out, tok_mid, tok_in))
    ):
        for i in range(1, ny):
            hop(k, out, mid, i).wait_send()

        def drain(i, carry, k=k, mid=mid, got=got):
            far(k, mid, got, i).wait_send()
            return carry

        lax.fori_loop(1, nz, drain, 0)
    for i in range(1, nt):
        gather(0, x_all, i).wait_send()
        gather(1, attn_all, i).wait_send()
        stat(i).wait_send()
        share(i).wait_send()


def body(
    patches,
    send_counts,
    window_ids,
    token_shard,
    first_gain,
    qkv_weight,
    out_weight,
    merge_gain,
    cotangent,
):
    bf16, f32 = jnp.bfloat16, jnp.float32
    dp, nt = lax.axis_size("dp"), lax.axis_size("tensor")
    ny = NY
    nz = dp // ny
    half = nz // 2
    rows_src, features = patches.shape
    rows_own = rows_src // 2
    lm_slots = cotangent.shape[0]
    lm_rows = 4 * lm_slots
    width = first_gain.shape[0]
    packed = qkv_weight.shape[1]
    cols = packed + features
    live = (width // 16) * (cols // 128)
    per = -(-(live + 1) // dp)
    tiles = window_ids.shape[0]
    ids = (window_ids + 4 * jnp.arange(tiles, dtype=jnp.int32)[:, None]).reshape(1, rows_own)
    vmem = pl.BlockSpec(memory_space=pltpu.VMEM)
    sems = pltpu.SemaphoreType.DMA

    def held(*shape, dtype=bf16):
        return pltpu.VMEM(shape, dtype)

    def legs(rows):
        out = held(ny, nz, rows, features)
        return [out, out, held(nz, ny, rows, features)]

    merged, qkv_grad, out_grad, gain_sum = pl.pallas_call(
        functools.partial(layer_kernel, nz, ny),
        out_shape=(
            jax.ShapeDtypeStruct((lm_rows, features), bf16),
            jax.ShapeDtypeStruct((width, packed), bf16),
            jax.ShapeDtypeStruct((width, features), bf16),
            jax.ShapeDtypeStruct((16, 128), f32),
        ),
        in_specs=[vmem] * 9,
        out_specs=(vmem,) * 4,
        scratch_shapes=[
            *legs(rows_src // dp),
            *legs(lm_rows // dp),
            *legs(lm_rows // dp),
            held(width, rows_own),
            held(width, rows_own),
            held(nt, 8, rows_own, dtype=f32),
            held(width, rows_own),
            held(nt, features, rows_own),
            held(packed, width),
            held(features, width),
            held(width, 1, dtype=f32),
            held(width, 2 * rows_own),
            held(cols, 2 * rows_own),
            held(16, 128, dtype=f32),
            sems((3, ny - 1)),
            sems((3, ny - 1)),
            sems((3, nz - 1)),
            sems((3, nz - 1)),
            sems((4, nt - 1)),
            sems((4, nt - 1)),
            held(per * dp, 16, 128),
            held(per * dp, 16, 128),
            held(nz, per, 16, 128),
            held(nz, per, 16, 128),
            held(nz, per, 16, 128),
            held(half, per, 16, 128),
            held(half, per, 16, 128),
            held(half, per, 16, 128),
            held(half, per, 16, 128),
            sems((3, nz)),
            sems((3, nz)),
            sems((2, half)),
            sems((2, half)),
            sems((2, half)),
            sems((2, half)),
            sems((3, nz)),
            sems((3, nz)),
        ],
        compiler_params=pltpu.CompilerParams(
            collective_id=0, has_side_effects=True, vmem_limit_bytes=56 * 1024 * 1024
        ),
        name="layer",
    )(
        patches,
        send_counts,
        ids,
        token_shard.reshape(dp, rows_own // 4),
        first_gain.reshape(1, width),
        qkv_weight,
        out_weight,
        merge_gain.reshape(1, features),
        cotangent.reshape(lm_rows, features),
    )
    return (
        merged.reshape(lm_slots, 4, features),
        qkv_grad,
        out_grad,
        gain_sum.reshape(-1)[:features],
    )


def solution(mesh):
    placed = (
        P("dp", "tensor"),
        P(),
        P("dp", None),
        P(),
        P(),
        P(None, "tensor"),
        P(None, "tensor"),
        P("tensor"),
        P("dp", None, "tensor"),
    )
    return jax.shard_map(
        body,
        mesh=mesh,
        in_specs=placed,
        out_specs=(P("dp", None, "tensor"), P(None, "tensor"), P(None, "tensor"), P("tensor")),
        check_vma=False,
    )
```

```python
import functools
import math

import jax
import jax.numpy as jnp
from jax import lax
from jax.experimental import pallas as pl
from jax.experimental.pallas import tpu as pltpu
from jax.sharding import PartitionSpec as P

HD = 80
WIN = 64
EPS = 1e-06
NY = 4
MESH = pl.DeviceIdType.MESH


def copy(src, dst, ss, rs, peer):
    return pltpu.make_async_remote_copy(
        src_ref=src, dst_ref=dst, send_sem=ss, recv_sem=rs, device_id=peer, device_id_type=MESH
    )


def iota(shape, dim):
    return lax.broadcasted_iota(jnp.int32, shape, dim)


def pick(cond):
    return jnp.where(cond, 1.0, 0.0).astype(jnp.bfloat16)


def to_row(col):
    n = col.shape[0]
    return jnp.sum(jnp.where(iota((n, n), 0) == iota((n, n), 1), col, 0.0), axis=0, keepdims=True)


def to_col(row):
    n = row.shape[1]
    return jnp.sum(jnp.where(iota((n, n), 0) == iota((n, n), 1), row, 0.0), axis=1, keepdims=True)


def dot(a, b, ca=1, cb=0):
    return lax.dot_general(a, b, (((ca,), (cb,)), ((), ())), preferred_element_type=jnp.float32)


def layer_kernel(
    nz,
    ny,
    patches_ref,
    counts_ref,
    ids_ref,
    tok_ref,
    gain1_ref,
    wqkv_t,
    wout_t,
    gain2_ref,
    cot_ref,
    merged_ref,
    qkv_ref,
    out_ref,
    gsum_ref,
    row_out,
    row_mid,
    row_in,
    cot_out,
    cot_mid,
    cot_in,
    tok_out,
    tok_mid,
    tok_in,
    x_all,
    attn_all,
    stat_all,
    spread,
    grad_in,
    wout,
    gain_col,
    lhs,
    lhs_in,
    rhs,
    rhs_in,
    part,
    near_in,
    class_sum,
    apart_in,
    full,
    hop_ss,
    hop_rs,
    far_ss,
    far_rs,
    t_ss,
    t_rs,
    y_ss,
    y_rs,
    z_ss,
    z_rs,
    g_ss,
    g_rs,
):
    bf16, f32 = jnp.bfloat16, jnp.float32
    dp = nz * ny
    nt = lax.axis_size("tensor")
    me = lax.axis_index("dp")
    rank = lax.axis_index("tensor")
    z, y = me // ny, lax.rem(me, ny)
    features, rows_src = patches_ref.shape
    rows_own = x_all.shape[1]
    width = x_all.shape[0]
    slot_cap = rows_src // dp
    lm_rows = 4 * cot_ref.shape[2]
    token_rows = lm_rows // dp
    token_cap = token_rows // 4
    tokens = rows_own // 4
    heads = wqkv_t.shape[0] // (3 * HD)
    groups = nz // 4
    scaling = 1.0 / math.sqrt(HD)
    log = lambda n: n.bit_length() - 1

    def dev(zz, yy):
        return {"dp": lax.rem(zz + nz, nz) * ny + lax.rem(yy + ny, ny)}

    def mate(i):
        return {"tensor": lax.rem(rank + i, nt)}

    barrier = pltpu.get_barrier_semaphore()
    for i in range(1, ny):
        pl.semaphore_signal(barrier, inc=1, device_id=dev(z, y + i), device_id_type=MESH)
    for i in range(1, nt):
        pl.semaphore_signal(barrier, inc=1, device_id=mate(i), device_id_type=MESH)
    for i in range(1, nz):
        pl.semaphore_signal(barrier, inc=1, device_id=dev(z + i, y), device_id_type=MESH)

    def owner_of(shape, dim, per):
        at = iota(shape, dim) >> log(per)
        return (at & (nz - 1)) * ny + (at >> log(nz))

    def hop(k, out, mid, i):
        to = lax.rem(y + i, ny)
        return copy(out.at[to], mid.at[y], hop_ss.at[k, i - 1], hop_rs.at[k, i - 1], dev(z, y + i))

    def far(k, mid, got, i):
        to = lax.rem(z + i, nz)
        return copy(
            mid.at[:, to], got.at[z], far_ss.at[k, i - 1], far_rs.at[k, i - 1], dev(z + i, y)
        )

    def first_hop(k, out, mid):
        for i in range(1, ny):
            hop(k, out, mid, i).start()
        mid[y] = out[y]

    def second_hop(k, out, mid, got):
        for i in range(1, ny):
            hop(k, out, mid, i).wait_recv()

        def send(i, carry):
            far(k, mid, got, i).start()
            return carry

        lax.fori_loop(1, nz, send, 0)
        got[z] = mid[:, z]

    def landed(k, mid, got):
        def take(i, carry):
            far(k, mid, got, i).wait_recv()
            return carry

        lax.fori_loop(1, nz, take, 0)

    n = rows_src
    own_row = counts_ref[pl.ds(me, 1), :].astype(f32)
    start = jnp.sum(
        jnp.where(iota((n, dp), 1) < owner_of((n, dp), 0, slot_cap), own_row, 0.0),
        axis=1,
        keepdims=True,
    ).astype(jnp.int32)
    slot = iota((n, 1), 0) & (slot_cap - 1)
    chosen = pick(iota((n, rows_src), 1) == jnp.minimum(start + slot, rows_src - 1))
    row_out[...] = dot(chosen, patches_ref[...], 1, 1).reshape(row_out.shape).astype(bf16)

    pl.semaphore_wait(barrier, ny - 1 + nt - 1 + nz - 1)
    first_hop(0, row_out, row_mid)

    lines = tok_ref.shape[1] // 128
    tok = jnp.concatenate([tok_ref[:, 128 * a : 128 * a + 128] for a in range(lines)], axis=0)
    tok = tok.astype(f32)
    per_line = log(128 // tokens)
    line = pick(iota((dp, lines), 1) == iota((dp, lines), 0) >> per_line)
    tok = dot(line, tok.astype(bf16))
    mine = (iota((dp, 128), 1) >> log(tokens)) == (iota((dp, 128), 0) & (128 // tokens - 1))
    named = jnp.logical_and(mine, tok == me.astype(f32))
    lm_row = to_row(jnp.sum(jnp.where(named, 1.0, 0.0), axis=1, keepdims=True))
    n = lm_rows
    start = jnp.sum(
        jnp.where(iota((n, dp), 1) < owner_of((n, dp), 0, token_rows), lm_row, 0.0),
        axis=1,
        keepdims=True,
    ).astype(jnp.int32)
    slot = (iota((n, 1), 0) & (token_rows - 1)) >> 2
    quarter = iota((n, 1), 0) & 3
    place = jnp.minimum(start + slot, lm_rows // 4 - 1)
    total = jnp.zeros((n, features), f32)
    for quart in range(4):
        place_q = jnp.where(quarter == quart, place, -1)
        total = total + dot(pick(iota((n, lm_rows // 4), 1) == place_q), cot_ref[quart], 1, 1)
    cot_out[...] = total.reshape(cot_out.shape).astype(bf16)

    second_hop(0, row_out, row_mid, row_in)
    first_hop(1, cot_out, cot_mid)

    n = rows_src
    sent_col = jnp.sum(
        jnp.where(iota((dp, dp), 1) == me, counts_ref[...].astype(f32), 0.0), axis=1, keepdims=True
    )
    sent_row = to_row(sent_col)
    source = iota((n, dp), 0) >> log(slot_cap)
    start = jnp.sum(jnp.where(iota((n, dp), 1) < source, sent_row, 0.0), axis=1, keepdims=True)
    count = jnp.sum(jnp.where(iota((n, dp), 1) == source, sent_row, 0.0), axis=1, keepdims=True)
    slot = iota((n, 1), 0) & (slot_cap - 1)
    where_to = jnp.where(slot < count.astype(jnp.int32), start.astype(jnp.int32) + slot, -1)
    placed = pick(iota((n, rows_own), 1) == where_to)

    second_hop(1, cot_out, cot_mid, cot_in)

    landed(0, row_mid, row_in)
    own = pl.ds(pl.multiple_of(rank * features, 16), features)
    arrived = row_in[...].astype(f32).reshape(rows_src, features).astype(bf16)
    x_own = dot(arrived, placed, 0, 0)
    x_all[own, :] = x_own.astype(bf16)

    def gather(k, buf, i):
        return copy(buf.at[own, :], buf.at[own, :], t_ss.at[k, i - 1], t_rs.at[k, i - 1], mate(i))

    for i in range(1, nt):
        gather(0, x_all, i).start()

    wout[...] = wout_t[...].T
    for b in range(width // 128):
        gain_col[128 * b : 128 * b + 128, :] = to_col(
            gain1_ref[128 * b : 128 * b + 128].reshape(1, 128)
        )
    merge_gain = to_col(gain2_ref[...])
    ids_col = jnp.concatenate(
        [to_col(ids_ref[a : a + 1, :].astype(f32)) + 4.0 * a for a in range(rows_own // WIN)], axis=0
    )
    same = ids_col == to_row(ids_col)

    own_line = jnp.sum(jnp.where(iota((dp, 128), 0) == me, tok, 0.0), axis=0, keepdims=True)
    at_lane = iota((tokens, 128), 0) + (me & (128 // tokens - 1)) * tokens
    target_col = jnp.sum(
        jnp.where(iota((tokens, 128), 1) == at_lane, own_line, 0.0), axis=1, keepdims=True
    )
    target = to_row(target_col)
    before = iota((tokens, tokens), 0) < iota((tokens, tokens), 1)
    order = jnp.sum(
        jnp.where(jnp.logical_and(target_col == target, before), 1.0, 0.0), axis=0, keepdims=True
    )
    token_slot = to_col(target * token_rows + order * 4)
    of_row = iota((tokens, rows_own), 1) >> 2
    slot_row = jnp.sum(
        jnp.where(iota((tokens, rows_own), 0) == of_row, token_slot, 0.0), axis=0, keepdims=True
    ).astype(jnp.int32) + (iota((1, rows_own), 1) & 3)
    taken = pick(iota((lm_rows, rows_own), 0) == slot_row)
    sent_id = owner_of((lm_rows, rows_own), 0, token_rows) * token_rows + (
        iota((lm_rows, rows_own), 0) & (token_rows - 1)
    )
    given = pick(sent_id == slot_row)

    for i in range(1, nt):
        gather(0, x_all, i).wait_recv()
    x = x_all[...].astype(f32)
    inv_first = lax.rsqrt(jnp.sum(x * x, axis=0, keepdims=True) / width + EPS)
    normed_in = (x * inv_first * gain_col[...]).astype(bf16)
    lhs[0] = normed_in

    def lend(kind, i):
        return copy(
            lhs.at[kind], lhs_in.at[y], y_ss.at[0, i - 1], y_rs.at[0, i - 1], dev(z, y + i)
        )

    def lend_to(kind):
        for i in range(1, ny):
            last = lax.rem(y + i, ny) == ny - 1

            @pl.when(last if kind else jnp.logical_not(last))
            def _(i=i):
                lend(kind, i).start()

    lend_to(0)
    packed = dot(wqkv_t[...], normed_in).astype(bf16)

    kept = []
    for h in range(heads):
        q, k, v = (packed[(3 * h + s) * HD : (3 * h + s + 1) * HD] for s in range(3))
        scores = jnp.where(same, dot(k, q, 0, 0) * scaling, -jnp.inf)
        raised = jnp.exp(scores - jnp.max(scores, axis=0, keepdims=True))
        weights = raised / jnp.sum(raised, axis=0, keepdims=True)
        rounded = weights.astype(bf16)
        at = pl.ds(pl.multiple_of(rank * features + h * HD, 16), HD)
        attn_all[at, :] = dot(v, rounded).astype(bf16)
        kept.append((q, k, v, weights, rounded))

    for i in range(1, nt):
        gather(1, attn_all, i).start()
    landed(1, cot_mid, cot_in)
    returned = cot_in[...].astype(f32).reshape(lm_rows, features).astype(bf16)
    upstream = dot(returned, taken, 0, 0)
    for i in range(1, nt):
        gather(1, attn_all, i).wait_recv()

    attn = attn_all[...]
    lhs[1] = attn
    lend_to(1)
    kind_here = jnp.where(y == ny - 1, 1, 0)
    lhs_in[y] = lhs[kind_here]
    residual = x_own + dot(wout_t[...], attn)
    lifted = merge_gain * upstream
    sums = [
        jnp.sum(residual * residual, axis=0, keepdims=True),
        jnp.sum(lifted * residual, axis=0, keepdims=True),
    ]
    stat_all[rank] = jnp.concatenate(sums + [jnp.zeros((6, rows_own), f32)], axis=0)

    def stat(i):
        at = stat_all.at[rank]
        return copy(at, at, t_ss.at[2, i - 1], t_rs.at[2, i - 1], mate(i))

    for i in range(1, nt):
        stat(i).start()
    for i in range(1, nt):
        stat(i).wait_recv()
    stats = jnp.sum(stat_all[...], axis=0)
    inv_second = lax.rsqrt(stats[0:1] / width + EPS)
    along = stats[1:2]
    scaled = residual * inv_second
    dresidual = (
        lifted * inv_second - residual * (along * (inv_second * inv_second * inv_second) / width)
    ).astype(bf16)
    spread[...] = dot(wout[...], dresidual).astype(bf16)

    def share(i):
        to = lax.rem(rank + i, nt)
        src = spread.at[pl.ds(pl.multiple_of(to * features, 16), features), :]
        return copy(src, grad_in.at[rank], t_ss.at[3, i - 1], t_rs.at[3, i - 1], mate(i))

    for i in range(1, nt):
        share(i).start()
    grad_in[rank] = spread[own, :]

    normed = (scaled * merge_gain).astype(bf16)
    tok_out[...] = dot(given, normed, 1, 1).reshape(tok_out.shape).astype(bf16)
    first_hop(2, tok_out, tok_mid)

    gains = jnp.sum(upstream * scaled, axis=1, keepdims=True)
    lane, sub = iota((features, 128), 1), iota((features, 128), 0)
    head = jnp.sum(jnp.where(lane == sub, gains, 0.0), axis=0, keepdims=True)
    tail = jnp.sum(jnp.where(lane + 128 == sub, gains, 0.0), axis=0, keepdims=True)
    gain_tile = jnp.concatenate([head, tail, jnp.zeros((14, 128), f32)], axis=0).astype(bf16)
    for s in range(ny):
        rhs[s, features : features + 16] = gain_tile
    rhs[ny - 1, 0:features] = dresidual

    second_hop(2, tok_out, tok_mid, tok_in)
    for i in range(1, nt):
        share(i).wait_recv()
    total = grad_in[0].astype(f32)
    for r in range(1, nt):
        total = total + grad_in[r].astype(f32)
    attn_grad = total.astype(bf16)

    for h in range(heads):
        q, k, v, weights, rounded = kept[h]
        g = attn_grad[h * HD : (h + 1) * HD]
        dprobs = dot(v, g, 0, 0)
        row_dot = jnp.sum(weights * dprobs, axis=0, keepdims=True)
        dscores = (weights * (dprobs - row_dot)).astype(bf16)
        grads = (
            (dot(k, dscores) * scaling).astype(bf16),
            (dot(q, dscores, 1, 1) * scaling).astype(bf16),
            dot(g, rounded, 1, 1).astype(bf16),
        )
        for s in range(3):
            line, half = (3 * h + s) // 2, (3 * h + s) % 2
            rhs[line, HD * half : HD * half + HD] = grads[s]

    def place_tokens():
        landed(2, tok_mid, tok_in)
        n = lm_rows
        owner = iota((n, dp), 0) >> log(token_rows)
        start = jnp.sum(jnp.where(iota((n, dp), 1) < owner, lm_row, 0.0), axis=1, keepdims=True)
        count = jnp.sum(jnp.where(iota((n, dp), 1) == owner, lm_row, 0.0), axis=1, keepdims=True)
        slot = (iota((n, 1), 0) & (token_rows - 1)) >> 2
        to = jnp.where(slot < count.astype(jnp.int32), start.astype(jnp.int32) + slot, -1)
        got = tok_in[...].astype(f32).reshape(n, features).astype(bf16)
        for quart in range(4):
            to_q = jnp.where((iota((n, 1), 0) & 3) == quart, to, -1)
            put = pick(iota((n, n // 4), 1) == to_q)
            merged_ref[quart] = dot(got, put, 0, 0).astype(bf16)

    def owed(i):
        to = lax.rem(y + i, ny)
        return copy(rhs.at[to], rhs_in.at[y], y_ss.at[1, i - 1], y_rs.at[1, i - 1], dev(z, y + i))

    for i in range(1, ny):
        owed(i).start()
    rhs_in[y] = rhs[y]
    live = (features // 16) * (width // 128)
    tiles = part.shape[0]
    per = tiles // nz
    block = per * groups
    part[pl.ds(live, tiles - live)] = jnp.zeros((tiles - live, 16, 128), bf16)
    for i in range(1, ny):
        lend(0, i).wait_recv()
    for i in range(1, ny):
        owed(i).wait_recv()
    left = jnp.concatenate([rhs_in[o, 0:features] for o in range(ny)], axis=1)
    for c in range(width // 128):
        right = jnp.concatenate([lhs_in[o, 128 * c : 128 * c + 128] for o in range(ny)], axis=1)
        lot = features // 16
        part[lot * c : lot * c + lot] = dot(left, right, 1, 1).astype(bf16).reshape(lot, 16, 128)
    gained = rhs_in[0, features : features + 16].astype(f32)
    for o in range(1, ny):
        gained = gained + rhs_in[o, features : features + 16].astype(f32)
    part[live] = gained.astype(bf16)

    steps = (2, 1, nz - 1)
    kin, place = lax.rem(z, 4), z // 4

    def class_of(step):
        return lax.rem(z + step, 4)

    def near(j):
        src = part.at[pl.ds(class_of(steps[j]) * block, block)]
        return copy(src, near_in.at[j], z_ss.at[0, j], z_rs.at[0, j], dev(z + steps[j], y))

    def apart(j):
        to = lax.rem(place + j, groups)
        src = class_sum.at[pl.ds(to * per, per)]
        return copy(
            src, apart_in.at[j - 1], z_ss.at[1, j - 1], z_rs.at[1, j - 1], dev(z + 4 * j, y)
        )

    for j in range(3):
        near(j).start()
    total = part[pl.ds(kin * block, block)].astype(f32)
    for j in range(3):
        near(j).wait_recv()
        total = total + near_in[j].astype(f32)
    class_sum[...] = total.astype(bf16)
    for j in range(1, groups):
        apart(j).start()
    total = class_sum[pl.ds(place * per, per)].astype(f32)
    for j in range(1, groups):
        apart(j).wait_recv()
        total = total + apart_in[j - 1].astype(f32)
    own_part = pl.ds(kin * block + place * per, per)
    full[y, own_part] = total.astype(bf16)

    def give_apart(j):
        at = full.at[y, own_part]
        return copy(at, at, g_ss.at[0, j - 1], g_rs.at[0, j - 1], dev(z + 4 * j, y))

    def give_near(j):
        at = full.at[y, pl.ds(kin * block, block)]
        return copy(at, at, g_ss.at[1, j], g_rs.at[1, j], dev(z + steps[j], y))

    def give_y(j, i):
        kind = kin if j == 3 else lax.rem(z + nz - steps[j], 4)
        at = full.at[y, pl.ds(kind * block, block)]
        return copy(at, at, g_ss.at[2 + j, i - 1], g_rs.at[2 + j, i - 1], dev(z, y + i))

    for j in range(1, groups):
        give_apart(j).start()
    place_tokens()
    for j in range(1, groups):
        give_apart(j).wait_recv()
    for j in (1, 2, 0):
        give_near(j).start()
    for i in range(1, ny):
        give_y(3, i).start()
    for j in (1, 2, 0):
        give_near(j).wait_recv()
        for i in range(1, ny):
            give_y(j, i).start()
    for j in (3, 1, 2, 0):
        for i in range(1, ny):
            give_y(j, i).wait_recv()

    lot = features // 16
    for s in range(ny):
        for c in range(width // 128):
            got = full[s, lot * c : lot * c + lot].reshape(features, 128)
            lanes = slice(128 * c, 128 * c + 128)
            if s < ny - 1:
                qkv_ref[features * s : features * s + features, lanes] = got
            else:
                out_ref[:, lanes] = got
    line = full[0, live].astype(f32)
    gsum_ref[:, 0:128] = line[0:1]
    gsum_ref[:, 128:features] = line[1:2, 0 : features - 128]

    for k, (out, mid, got) in enumerate(
        ((row_out, row_mid, row_in), (cot_out, cot_mid, cot_in), (tok_out, tok_mid, tok_in))
    ):
        for i in range(1, ny):
            hop(k, out, mid, i).wait_send()

        def drain(i, carry, k=k, mid=mid, got=got):
            far(k, mid, got, i).wait_send()
            return carry

        lax.fori_loop(1, nz, drain, 0)
    for i in range(1, nt):
        gather(0, x_all, i).wait_send()
        gather(1, attn_all, i).wait_send()
        stat(i).wait_send()
        share(i).wait_send()
    for i in range(1, ny):
        lend(0, i).wait_send()
        owed(i).wait_send()
        for j in range(4):
            give_y(j, i).wait_send()
    for j in range(3):
        near(j).wait_send()
        give_near(j).wait_send()
    for j in range(1, groups):
        apart(j).wait_send()
        give_apart(j).wait_send()


def body(
    patches,
    send_counts,
    window_ids,
    token_shard,
    first_gain,
    qkv_weight,
    out_weight,
    merge_gain,
    cotangent,
):
    bf16, f32 = jnp.bfloat16, jnp.float32
    dp, nt = lax.axis_size("dp"), lax.axis_size("tensor")
    ny = NY
    nz = dp // ny
    rows_src, features = patches.shape
    rows_own = rows_src // 2
    lm_slots = cotangent.shape[0]
    lm_rows = 4 * lm_slots
    width = first_gain.shape[0]
    packed = qkv_weight.shape[1]
    live = (features // 16) * (width // 128)
    per = -(-(live + 1) // nz)
    groups = nz // 4
    vmem = pl.BlockSpec(memory_space=pltpu.VMEM)
    sems = pltpu.SemaphoreType.DMA

    def held(*shape, dtype=bf16):
        return pltpu.VMEM(shape, dtype)

    def legs(rows):
        out = held(ny, nz, rows, features)
        return [out, out, held(nz, ny, rows, features)]

    merged, qkv_grad, out_grad, gain_sum = pl.pallas_call(
        functools.partial(layer_kernel, nz, ny),
        out_shape=(
            jax.ShapeDtypeStruct((4, features, lm_slots), bf16),
            jax.ShapeDtypeStruct((packed, width), bf16),
            jax.ShapeDtypeStruct((features, width), bf16),
            jax.ShapeDtypeStruct((1, features), f32),
        ),
        in_specs=[vmem] * 9,
        out_specs=(vmem,) * 4,
        scratch_shapes=[
            *legs(rows_src // dp),
            *legs(lm_rows // dp),
            *legs(lm_rows // dp),
            held(width, rows_own),
            held(width, rows_own),
            held(nt, 8, rows_own, dtype=f32),
            held(width, rows_own),
            held(nt, features, rows_own),
            held(width, features),
            held(width, 1, dtype=f32),
            held(2, width, rows_own),
            held(ny, width, rows_own),
            held(ny, features + 16, rows_own),
            held(ny, features + 16, rows_own),
            held(per * nz, 16, 128),
            held(3, per * groups, 16, 128),
            held(per * groups, 16, 128),
            held(max(groups - 1, 1), per, 16, 128),
            held(ny, per * nz, 16, 128),
            sems((3, ny - 1)),
            sems((3, ny - 1)),
            sems((3, nz - 1)),
            sems((3, nz - 1)),
            sems((4, nt - 1)),
            sems((4, nt - 1)),
            sems((2, ny - 1)),
            sems((2, ny - 1)),
            sems((2, 3)),
            sems((2, 3)),
            sems((6, 3)),
            sems((6, 3)),
        ],
        compiler_params=pltpu.CompilerParams(
            collective_id=0, has_side_effects=True, vmem_limit_bytes=56 * 1024 * 1024
        ),
        name="layer",
    )(
        patches.T,
        send_counts,
        window_ids,
        token_shard.reshape(1, token_shard.shape[0]),
        first_gain,
        qkv_weight.T,
        out_weight.T,
        merge_gain.reshape(1, features),
        cotangent.transpose(1, 2, 0),
    )
    return (
        merged.transpose(2, 0, 1),
        qkv_grad.T,
        out_grad.T,
        gain_sum.reshape(features),
    )


def solution(mesh):
    placed = (
        P("dp", "tensor"),
        P(),
        P("dp", None),
        P(),
        P(),
        P(None, "tensor"),
        P(None, "tensor"),
        P("tensor"),
        P("dp", None, "tensor"),
    )
    return jax.shard_map(
        body,
        mesh=mesh,
        in_specs=placed,
        out_specs=(P("dp", None, "tensor"), P(None, "tensor"), P(None, "tensor"), P("tensor")),
        check_vma=False,
    )
```

```python
import functools
import math

import jax
import jax.numpy as jnp
from jax import lax
from jax.experimental import pallas as pl
from jax.experimental.pallas import tpu as pltpu
from jax.sharding import PartitionSpec as P

HD = 80
WIN = 64
EPS = 1e-06
NY = 4
MESH = pl.DeviceIdType.MESH


def copy(src, dst, ss, rs, peer):
    return pltpu.make_async_remote_copy(
        src_ref=src, dst_ref=dst, send_sem=ss, recv_sem=rs, device_id=peer, device_id_type=MESH
    )


def iota(shape, dim):
    return lax.broadcasted_iota(jnp.int32, shape, dim)


def pick(cond):
    return jnp.where(cond, 1.0, 0.0).astype(jnp.bfloat16)


def to_row(col):
    n = col.shape[0]
    return jnp.sum(jnp.where(iota((n, n), 0) == iota((n, n), 1), col, 0.0), axis=0, keepdims=True)


def to_col(row):
    n = row.shape[1]
    return jnp.sum(jnp.where(iota((n, n), 0) == iota((n, n), 1), row, 0.0), axis=1, keepdims=True)


def dot(a, b, ca=1, cb=0):
    return lax.dot_general(a, b, (((ca,), (cb,)), ((), ())), preferred_element_type=jnp.float32)


def layer_kernel(
    nz,
    ny,
    patches_ref,
    counts_ref,
    ids_ref,
    tok_ref,
    gain1_ref,
    wqkv_t,
    wout_t,
    gain2_ref,
    cot_ref,
    merged_ref,
    tiles_ref,
    row_out,
    row_mid,
    row_in,
    cot_out,
    cot_mid,
    cot_in,
    tok_out,
    tok_mid,
    tok_in,
    x_all,
    attn_all,
    stat_all,
    spread,
    grad_in,
    wout,
    gain_col,
    lhs,
    lhs_in,
    rhs,
    rhs_in,
    part,
    near_in,
    class_sum,
    apart_in,
    full,
    hop_ss,
    hop_rs,
    far_ss,
    far_rs,
    t_ss,
    t_rs,
    y_ss,
    y_rs,
    z_ss,
    z_rs,
    g_ss,
    g_rs,
):
    bf16, f32 = jnp.bfloat16, jnp.float32
    dp = nz * ny
    nt = lax.axis_size("tensor")
    me = lax.axis_index("dp")
    rank = lax.axis_index("tensor")
    z, y = me // ny, lax.rem(me, ny)
    features, rows_src = patches_ref.shape
    rows_own = x_all.shape[1]
    width = x_all.shape[0]
    slot_cap = rows_src // dp
    lm_rows = 4 * cot_ref.shape[2]
    token_rows = lm_rows // dp
    token_cap = token_rows // 4
    tokens = rows_own // 4
    heads = wqkv_t.shape[0] // (3 * HD)
    groups = nz // 4
    scaling = 1.0 / math.sqrt(HD)
    log = lambda n: n.bit_length() - 1

    def dev(zz, yy):
        return {"dp": lax.rem(zz + nz, nz) * ny + lax.rem(yy + ny, ny)}

    def mate(i):
        return {"tensor": lax.rem(rank + i, nt)}

    barrier = pltpu.get_barrier_semaphore()
    distant = sorted(range(1, nz), key=lambda i: -min(i, nz - i))
    plain = list(range(1, nz))
    for i in distant:
        pl.semaphore_signal(barrier, inc=1, device_id=dev(z + i, y), device_id_type=MESH)
    for i in range(1, ny):
        pl.semaphore_signal(barrier, inc=1, device_id=dev(z, y + i), device_id_type=MESH)
    for i in range(1, nt):
        pl.semaphore_signal(barrier, inc=1, device_id=mate(i), device_id_type=MESH)

    def owner_of(shape, dim, per):
        at = iota(shape, dim) >> log(per)
        return (at & (nz - 1)) * ny + (at >> log(nz))

    def hop(k, out, mid, i):
        to = lax.rem(y + i, ny)
        return copy(out.at[to], mid.at[y], hop_ss.at[k, i - 1], hop_rs.at[k, i - 1], dev(z, y + i))

    def far(k, mid, got, i):
        to = lax.rem(z + i, nz)
        return copy(
            mid.at[:, to], got.at[z], far_ss.at[k, i - 1], far_rs.at[k, i - 1], dev(z + i, y)
        )

    def first_hop(k, out, mid):
        for i in range(1, ny):
            hop(k, out, mid, i).start()
        mid[y] = out[y]

    def onward(k, mid, got, order):
        for i in order:
            far(k, mid, got, i).start()

    def second_hop(k, out, mid, got, order):
        for i in range(1, ny):
            hop(k, out, mid, i).wait_recv()
        onward(k, mid, got, order)
        got[z] = mid[:, z]

    def landed(k, mid, got):
        def take(i, carry):
            far(k, mid, got, i).wait_recv()
            return carry

        lax.fori_loop(1, nz, take, 0)

    n = rows_src
    own_row = counts_ref[pl.ds(me, 1), :].astype(f32)
    start = jnp.sum(
        jnp.where(iota((n, dp), 1) < owner_of((n, dp), 0, slot_cap), own_row, 0.0),
        axis=1,
        keepdims=True,
    ).astype(jnp.int32)
    slot = iota((n, 1), 0) & (slot_cap - 1)
    chosen = pick(iota((n, rows_src), 1) == jnp.minimum(start + slot, rows_src - 1))
    row_out[...] = dot(chosen, patches_ref[...], 1, 1).reshape(row_out.shape).astype(bf16)

    lines = tok_ref.shape[1] // 128
    tok = jnp.concatenate([tok_ref[:, 128 * a : 128 * a + 128] for a in range(lines)], axis=0)
    tok = tok.astype(f32)
    per_line = log(128 // tokens)
    line = pick(iota((dp, lines), 1) == iota((dp, lines), 0) >> per_line)
    tok = dot(line, tok.astype(bf16))
    mine = (iota((dp, 128), 1) >> log(tokens)) == (iota((dp, 128), 0) & (128 // tokens - 1))
    named = jnp.logical_and(mine, tok == me.astype(f32))
    lm_row = to_row(jnp.sum(jnp.where(named, 1.0, 0.0), axis=1, keepdims=True))
    n = lm_rows
    start = jnp.sum(
        jnp.where(iota((n, dp), 1) < owner_of((n, dp), 0, token_rows), lm_row, 0.0),
        axis=1,
        keepdims=True,
    ).astype(jnp.int32)
    slot = (iota((n, 1), 0) & (token_rows - 1)) >> 2
    quarter = iota((n, 1), 0) & 3
    place = jnp.minimum(start + slot, lm_rows // 4 - 1)
    total = jnp.zeros((n, features), f32)
    for quart in range(4):
        place_q = jnp.where(quarter == quart, place, -1)
        total = total + dot(pick(iota((n, lm_rows // 4), 1) == place_q), cot_ref[quart], 1, 1)
    cot_out[...] = total.reshape(cot_out.shape).astype(bf16)

    pl.semaphore_wait(barrier, ny - 1 + nt - 1 + nz - 1)
    first_hop(0, row_out, row_mid)
    second_hop(0, row_out, row_mid, row_in, plain)
    first_hop(1, cot_out, cot_mid)

    n = rows_src
    sent_col = jnp.sum(
        jnp.where(iota((dp, dp), 1) == me, counts_ref[...].astype(f32), 0.0), axis=1, keepdims=True
    )
    sent_row = to_row(sent_col)
    source = iota((n, dp), 0) >> log(slot_cap)
    start = jnp.sum(jnp.where(iota((n, dp), 1) < source, sent_row, 0.0), axis=1, keepdims=True)
    count = jnp.sum(jnp.where(iota((n, dp), 1) == source, sent_row, 0.0), axis=1, keepdims=True)
    slot = iota((n, 1), 0) & (slot_cap - 1)
    where_to = jnp.where(slot < count.astype(jnp.int32), start.astype(jnp.int32) + slot, -1)
    placed = pick(iota((n, rows_own), 1) == where_to)

    second_hop(1, cot_out, cot_mid, cot_in, plain)

    landed(0, row_mid, row_in)
    own = pl.ds(pl.multiple_of(rank * features, 16), features)
    arrived = row_in[...].astype(f32).reshape(rows_src, features).astype(bf16)
    x_own = dot(arrived, placed, 0, 0)
    x_all[own, :] = x_own.astype(bf16)

    def gather(k, buf, i):
        return copy(buf.at[own, :], buf.at[own, :], t_ss.at[k, i - 1], t_rs.at[k, i - 1], mate(i))

    for i in range(1, nt):
        gather(0, x_all, i).start()

    wout[...] = wout_t[...].T
    for b in range(width // 128):
        gain_col[128 * b : 128 * b + 128, :] = to_col(
            gain1_ref[128 * b : 128 * b + 128].reshape(1, 128)
        )
    merge_gain = to_col(gain2_ref[...])
    ids_col = jnp.concatenate(
        [to_col(ids_ref[a : a + 1, :].astype(f32)) + 4.0 * a for a in range(rows_own // WIN)], axis=0
    )
    same = ids_col == to_row(ids_col)

    own_line = jnp.sum(jnp.where(iota((dp, 128), 0) == me, tok, 0.0), axis=0, keepdims=True)
    at_lane = iota((tokens, 128), 0) + (me & (128 // tokens - 1)) * tokens
    target_col = jnp.sum(
        jnp.where(iota((tokens, 128), 1) == at_lane, own_line, 0.0), axis=1, keepdims=True
    )
    target = to_row(target_col)
    before = iota((tokens, tokens), 0) < iota((tokens, tokens), 1)
    order = jnp.sum(
        jnp.where(jnp.logical_and(target_col == target, before), 1.0, 0.0), axis=0, keepdims=True
    )
    token_slot = to_col(target * token_rows + order * 4)
    of_row = iota((tokens, rows_own), 1) >> 2
    slot_row = jnp.sum(
        jnp.where(iota((tokens, rows_own), 0) == of_row, token_slot, 0.0), axis=0, keepdims=True
    ).astype(jnp.int32) + (iota((1, rows_own), 1) & 3)
    taken = pick(iota((lm_rows, rows_own), 0) == slot_row)
    sent_id = owner_of((lm_rows, rows_own), 0, token_rows) * token_rows + (
        iota((lm_rows, rows_own), 0) & (token_rows - 1)
    )
    given = pick(sent_id == slot_row)

    for i in range(1, nt):
        gather(0, x_all, i).wait_recv()
    x = x_all[...].astype(f32)
    inv_first = lax.rsqrt(jnp.sum(x * x, axis=0, keepdims=True) / width + EPS)
    normed_in = (x * inv_first * gain_col[...]).astype(bf16)
    lhs[0] = normed_in

    def lend(kind, i):
        return copy(
            lhs.at[kind], lhs_in.at[y], y_ss.at[0, i - 1], y_rs.at[0, i - 1], dev(z, y + i)
        )

    def lend_to(kind):
        for i in range(1, ny):
            last = lax.rem(y + i, ny) == ny - 1

            @pl.when(last if kind else jnp.logical_not(last))
            def _(i=i):
                lend(kind, i).start()

    lend_to(0)
    packed = dot(wqkv_t[...], normed_in).astype(bf16)

    kept = []
    for h in range(heads):
        q, k, v = (packed[(3 * h + s) * HD : (3 * h + s + 1) * HD] for s in range(3))
        scores = jnp.where(same, dot(k, q, 0, 0) * scaling, -jnp.inf)
        raised = jnp.exp(scores - jnp.max(scores, axis=0, keepdims=True))
        weights = raised / jnp.sum(raised, axis=0, keepdims=True)
        rounded = weights.astype(bf16)
        at = pl.ds(pl.multiple_of(rank * features + h * HD, 16), HD)
        attn_all[at, :] = dot(v, rounded).astype(bf16)
        kept.append((q, k, v, weights, rounded))

    for i in range(1, nt):
        gather(1, attn_all, i).start()
    landed(1, cot_mid, cot_in)
    returned = cot_in[...].astype(f32).reshape(lm_rows, features).astype(bf16)
    upstream = dot(returned, taken, 0, 0)
    for i in range(1, nt):
        gather(1, attn_all, i).wait_recv()

    attn = attn_all[...]
    lhs[1] = attn
    lend_to(1)
    kind_here = jnp.where(y == ny - 1, 1, 0)
    lhs_in[y] = lhs[kind_here]
    residual = x_own + dot(wout_t[...], attn)
    lifted = merge_gain * upstream
    sums = [
        jnp.sum(residual * residual, axis=0, keepdims=True),
        jnp.sum(lifted * residual, axis=0, keepdims=True),
    ]
    stat_all[rank] = jnp.concatenate(sums + [jnp.zeros((6, rows_own), f32)], axis=0)

    def stat(i):
        at = stat_all.at[rank]
        return copy(at, at, t_ss.at[2, i - 1], t_rs.at[2, i - 1], mate(i))

    for i in range(1, nt):
        stat(i).start()
    for i in range(1, nt):
        stat(i).wait_recv()
    stats = jnp.sum(stat_all[...], axis=0)
    inv_second = lax.rsqrt(stats[0:1] / width + EPS)
    along = stats[1:2]
    scaled = residual * inv_second
    dresidual = (
        lifted * inv_second - residual * (along * (inv_second * inv_second * inv_second) / width)
    ).astype(bf16)
    spread[...] = dot(wout[...], dresidual).astype(bf16)

    def share(i):
        to = lax.rem(rank + i, nt)
        src = spread.at[pl.ds(pl.multiple_of(to * features, 16), features), :]
        return copy(src, grad_in.at[rank], t_ss.at[3, i - 1], t_rs.at[3, i - 1], mate(i))

    for i in range(1, nt):
        share(i).start()
    grad_in[rank] = spread[own, :]

    normed = (scaled * merge_gain).astype(bf16)
    tok_out[...] = dot(given, normed, 1, 1).reshape(tok_out.shape).astype(bf16)
    first_hop(2, tok_out, tok_mid)

    gains = jnp.sum(upstream * scaled, axis=1, keepdims=True)
    lane, sub = iota((features, 128), 1), iota((features, 128), 0)
    head = jnp.sum(jnp.where(lane == sub, gains, 0.0), axis=0, keepdims=True)
    tail = jnp.sum(jnp.where(lane + 128 == sub, gains, 0.0), axis=0, keepdims=True)
    gain_tile = jnp.concatenate([head, tail, jnp.zeros((14, 128), f32)], axis=0).astype(bf16)
    for s in range(ny):
        rhs[s, features : features + 16] = gain_tile
    rhs[ny - 1, 0:features] = dresidual

    split = 5
    second_hop(2, tok_out, tok_mid, tok_in, distant[:split])
    for i in range(1, nt):
        share(i).wait_recv()
    total = grad_in[0].astype(f32)
    for r in range(1, nt):
        total = total + grad_in[r].astype(f32)
    attn_grad = total.astype(bf16)

    for h in range(heads):
        q, k, v, weights, rounded = kept[h]
        g = attn_grad[h * HD : (h + 1) * HD]
        dprobs = dot(v, g, 0, 0)
        row_dot = jnp.sum(weights * dprobs, axis=0, keepdims=True)
        dscores = (weights * (dprobs - row_dot)).astype(bf16)
        grads = (
            (dot(k, dscores) * scaling).astype(bf16),
            (dot(q, dscores, 1, 1) * scaling).astype(bf16),
            dot(g, rounded, 1, 1).astype(bf16),
        )
        for s in range(3):
            line, half = (3 * h + s) // 2, (3 * h + s) % 2
            rhs[line, HD * half : HD * half + HD] = grads[s]

    def place_tokens():
        landed(2, tok_mid, tok_in)
        n = lm_rows
        owner = iota((n, dp), 0) >> log(token_rows)
        start = jnp.sum(jnp.where(iota((n, dp), 1) < owner, lm_row, 0.0), axis=1, keepdims=True)
        count = jnp.sum(jnp.where(iota((n, dp), 1) == owner, lm_row, 0.0), axis=1, keepdims=True)
        slot = (iota((n, 1), 0) & (token_rows - 1)) >> 2
        to = jnp.where(slot < count.astype(jnp.int32), start.astype(jnp.int32) + slot, -1)
        got = tok_in[...].astype(f32).reshape(n, features).astype(bf16)
        for quart in range(4):
            to_q = jnp.where((iota((n, 1), 0) & 3) == quart, to, -1)
            put = pick(iota((n, n // 4), 1) == to_q)
            merged_ref[quart] = dot(got, put, 0, 0).astype(bf16)

    def owed(i):
        to = lax.rem(y + i, ny)
        return copy(rhs.at[to], rhs_in.at[y], y_ss.at[1, i - 1], y_rs.at[1, i - 1], dev(z, y + i))

    for i in range(1, ny):
        owed(i).start()
    rhs_in[y] = rhs[y]
    live = (features // 16) * (width // 128)
    tiles = part.shape[0]
    per = tiles // nz
    block = per * groups
    part[pl.ds(live, tiles - live)] = jnp.zeros((tiles - live, 16, 128), bf16)
    for i in range(1, ny):
        lend(0, i).wait_recv()
    for i in range(1, ny):
        owed(i).wait_recv()
    left = jnp.concatenate([rhs_in[o, 0:features] for o in range(ny)], axis=1)
    for c in range(width // 128):
        right = jnp.concatenate([lhs_in[o, 128 * c : 128 * c + 128] for o in range(ny)], axis=1)
        lot = features // 16
        part[lot * c : lot * c + lot] = dot(left, right, 1, 1).astype(bf16).reshape(lot, 16, 128)
    gained = rhs_in[0, features : features + 16].astype(f32)
    for o in range(1, ny):
        gained = gained + rhs_in[o, features : features + 16].astype(f32)
    part[live] = gained.astype(bf16)

    steps = (2, 1, nz - 1)
    kin, place = lax.rem(z, 4), z // 4

    def class_of(step):
        return lax.rem(z + step, 4)

    def chunk(kind, group):
        return pl.ds(kind * block + group * per, per)

    def turn(zz, o):
        return lax.rem(lax.rem(zz + nz, nz) // 4 + o, groups)

    def near(j, group):
        return copy(
            part.at[chunk(class_of(steps[j]), group)],
            near_in.at[group, j],
            z_ss.at[j, group],
            z_rs.at[j, group],
            dev(z + steps[j], y),
        )

    def apart(o):
        src = class_sum.at[turn(z, o)]
        return copy(
            src, apart_in.at[o - 1], z_ss.at[3, o - 1], z_rs.at[3, o - 1], dev(z + 4 * o, y)
        )

    outward = sorted(range(groups), key=lambda o: min(o, groups - o))
    inward = outward[::-1]
    for o in inward:
        for j in range(3):
            near(j, turn(z + steps[j], o)).start()
    for o in inward:
        group = turn(z, o)
        total = part[chunk(kin, group)].astype(f32)
        for j in range(3):
            near(j, group).wait_recv()
            total = total + near_in[group, j].astype(f32)
        if o:
            class_sum[group] = total.astype(bf16)
            apart(o).start()
    onward(2, tok_mid, tok_in, distant[split:])
    for o in inward[:-1]:
        apart(o).wait_recv()
        total = total + apart_in[o - 1].astype(f32)
    full[y, chunk(kin, place)] = total.astype(bf16)

    def give_apart(o):
        at = full.at[y, chunk(kin, place)]
        return copy(at, at, g_ss.at[0, o - 1], g_rs.at[0, o - 1], dev(z + 4 * o, y))

    def give_near(o, j):
        at = full.at[y, chunk(kin, turn(z, groups - o))]
        return copy(at, at, g_ss.at[1 + o, j], g_rs.at[1 + o, j], dev(z + steps[j], y))

    def give_y(o, j, i):
        zz = z if j == 3 else z - steps[j]
        at = full.at[y, chunk(lax.rem(zz + nz, 4), turn(zz, groups - o))]
        k = 1 + groups + 4 * o + j
        return copy(at, at, g_ss.at[k, i - 1], g_rs.at[k, i - 1], dev(z, y + i))

    def send_on(o):
        for j in (1, 2, 0):
            give_near(o, j).start()
        for i in range(1, ny):
            give_y(o, 3, i).start()

    def from_near(o):
        for j in (1, 2, 0):
            give_near(o, j).wait_recv()
            for i in range(1, ny):
                give_y(o, j, i).start()

    for o in inward[:-1]:
        give_apart(o).start()
    send_on(0)
    from_near(0)
    for o in outward[1:-1]:
        give_apart(o).wait_recv()
        send_on(o)
    for o in outward[1:-1]:
        from_near(o)
    for o in outward[1:][-1:]:
        give_apart(o).wait_recv()
        send_on(o)
        from_near(o)
    place_tokens()
    for o in outward:
        for j in (3, 1, 2, 0):
            for i in range(1, ny):
                give_y(o, j, i).wait_recv()

    tiles_ref[...] = full[...]

    for k, (out, mid, got) in enumerate(
        ((row_out, row_mid, row_in), (cot_out, cot_mid, cot_in), (tok_out, tok_mid, tok_in))
    ):
        for i in range(1, ny):
            hop(k, out, mid, i).wait_send()

        def drain(i, carry, k=k, mid=mid, got=got):
            far(k, mid, got, i).wait_send()
            return carry

        lax.fori_loop(1, nz, drain, 0)
    for i in range(1, nt):
        gather(0, x_all, i).wait_send()
        gather(1, attn_all, i).wait_send()
        stat(i).wait_send()
        share(i).wait_send()
    for i in range(1, ny):
        lend(0, i).wait_send()
        owed(i).wait_send()
        for o in range(groups):
            for j in range(4):
                give_y(o, j, i).wait_send()
    for o in range(groups):
        for j in range(3):
            near(j, turn(z + steps[j], o)).wait_send()
            give_near(o, j).wait_send()
    for o in range(1, groups):
        apart(o).wait_send()
        give_apart(o).wait_send()


def spread_kernel(tiles_ref, merged_ref, placed_ref, qkv_ref, out_ref, gsum_ref):
    ny, tiles = tiles_ref.shape[0], tiles_ref.shape[1]
    features, width = out_ref.shape
    lot = features // 16
    live = lot * (width // 128)
    for s in range(ny):
        for c in range(width // 128):
            got = tiles_ref[s, lot * c : lot * c + lot].reshape(features, 128)
            lanes = slice(128 * c, 128 * c + 128)
            if s < ny - 1:
                qkv_ref[features * s : features * s + features, lanes] = got
            else:
                out_ref[:, lanes] = got
    line = tiles_ref[0, live].astype(jnp.float32)
    gsum_ref[:, 0:128] = line[0:1]
    gsum_ref[:, 128:features] = line[1:2, 0 : features - 128]
    placed_ref[...] = merged_ref[...]


def body(
    patches,
    send_counts,
    window_ids,
    token_shard,
    first_gain,
    qkv_weight,
    out_weight,
    merge_gain,
    cotangent,
):
    bf16, f32 = jnp.bfloat16, jnp.float32
    dp, nt = lax.axis_size("dp"), lax.axis_size("tensor")
    ny = NY
    nz = dp // ny
    rows_src, features = patches.shape
    rows_own = rows_src // 2
    lm_slots = cotangent.shape[0]
    lm_rows = 4 * lm_slots
    width = first_gain.shape[0]
    packed = qkv_weight.shape[1]
    live = (features // 16) * (width // 128)
    per = -(-(live + 1) // nz)
    groups = nz // 4
    vmem = pl.BlockSpec(memory_space=pltpu.VMEM)
    sems = pltpu.SemaphoreType.DMA

    def held(*shape, dtype=bf16):
        return pltpu.VMEM(shape, dtype)

    def legs(rows):
        out = held(ny, nz, rows, features)
        return [out, out, held(nz, ny, rows, features)]

    merged, tiles = pl.pallas_call(
        functools.partial(layer_kernel, nz, ny),
        out_shape=(
            jax.ShapeDtypeStruct((4, features, lm_slots), bf16),
            jax.ShapeDtypeStruct((ny, per * nz, 16, 128), bf16),
        ),
        in_specs=[vmem] * 9,
        out_specs=(vmem,) * 2,
        scratch_shapes=[
            *legs(rows_src // dp),
            *legs(lm_rows // dp),
            *legs(lm_rows // dp),
            held(width, rows_own),
            held(width, rows_own),
            held(nt, 8, rows_own, dtype=f32),
            held(width, rows_own),
            held(nt, features, rows_own),
            held(width, features),
            held(width, 1, dtype=f32),
            held(2, width, rows_own),
            held(ny, width, rows_own),
            held(ny, features + 16, rows_own),
            held(ny, features + 16, rows_own),
            held(per * nz, 16, 128),
            held(groups, 3, per, 16, 128),
            held(groups, per, 16, 128),
            held(max(groups - 1, 1), per, 16, 128),
            held(ny, per * nz, 16, 128),
            sems((3, ny - 1)),
            sems((3, ny - 1)),
            sems((3, nz - 1)),
            sems((3, nz - 1)),
            sems((4, nt - 1)),
            sems((4, nt - 1)),
            sems((2, ny - 1)),
            sems((2, ny - 1)),
            sems((4, max(groups, 3))),
            sems((4, max(groups, 3))),
            sems((1 + 5 * groups, 3)),
            sems((1 + 5 * groups, 3)),
        ],
        compiler_params=pltpu.CompilerParams(
            collective_id=0, has_side_effects=True, vmem_limit_bytes=56 * 1024 * 1024
        ),
        name="layer",
    )(
        patches.T,
        send_counts,
        window_ids,
        token_shard.reshape(1, token_shard.shape[0]),
        first_gain,
        qkv_weight.T,
        out_weight.T,
        merge_gain.reshape(1, features),
        cotangent.transpose(1, 2, 0),
    )
    merged, qkv_grad, out_grad, gain_sum = pl.pallas_call(
        spread_kernel,
        out_shape=(
            jax.ShapeDtypeStruct((4, features, lm_slots), bf16),
            jax.ShapeDtypeStruct((packed, width), bf16),
            jax.ShapeDtypeStruct((features, width), bf16),
            jax.ShapeDtypeStruct((1, features), f32),
        ),
        in_specs=[vmem] * 2,
        out_specs=(vmem,) * 4,
        name="spread",
    )(tiles, merged)
    return (
        merged.transpose(2, 0, 1),
        qkv_grad.T,
        out_grad.T,
        gain_sum.reshape(features),
    )


def solution(mesh):
    placed = (
        P("dp", "tensor"),
        P(),
        P("dp", None),
        P(),
        P(),
        P(None, "tensor"),
        P(None, "tensor"),
        P("tensor"),
        P("dp", None, "tensor"),
    )
    return jax.shard_map(
        body,
        mesh=mesh,
        in_specs=placed,
        out_specs=(P("dp", None, "tensor"), P(None, "tensor"), P(None, "tensor"), P("tensor")),
        check_vma=False,
    )
```
